128 devices in a mesh: dp: 8 (over z_hi, y), vocab: 16 (over x, z_lo, core).
Axes of the slice: x: 4, y: 4, z: 4 (z_hi: 2, z_lo: 2; z = z_hi * 2 + z_lo), core: 2. Of those that a mesh axis runs over, the one named last changes fastest.
Arguments:
- start_hidden: bfloat16 [512, 3072], P('dp'), may hold values from -10.464474 to 10.464474
- offsets: bfloat16 [512, 3072], P('dp'), may hold values from -1.8042196 to 1.8042196
- norm_gain: float32 [3072], replicated, may hold values from 0.5 to 1.5
- head_table: bfloat16 [131072, 3072], P(('dp', 'vocab')), may hold values from -0.3969283 to 0.3969283
- targets_one: int32 [512], replicated, may hold values from 0 to 131071
- targets_two: int32 [512], replicated, may hold values from 0 to 131071
- advantage: int32 [512], replicated, may hold values from -2 to 2
Outputs:
- head_grad: float32 [131072, 3072], P(('dp', 'vocab'))
- gain_grad: float32 [3072], replicated
- offset_grad: bfloat16 [512, 3072], P('dp')
The draws below stay inside these ranges and needn't reach their ends.
All inputs are finite; a program needn't handle non-finite values.
Results may differ from the reference program's by a relative error of at most 0.009.
Values may be sent and summed in bfloat16 or wider, within the bound.
No kernel may reach another device: no remote copies, remote signals or barrier semaphores. Data moves between devices by JAX's collectives and lax.ppermute only.
A program may use at most 128 MiB of HBM per device.

```python
import jax
import jax.numpy as jnp
from jax import lax

D = 3072
VOCAB = 131072
ROLLOUTS = 512


def shared_table(key):
    spread = 3.3 / D ** 0.5
    base = jnp.clip(jax.random.normal(jax.random.fold_in(key, 11), (VOCAB, D), jnp.float32), -5.0, 5.0) * spread
    return (base, spread)


def draw_head_table(key, part):
    base, spread = shared_table(key)
    table = base
    return table.astype(jnp.bfloat16)


def draw_start_hidden(key, part):
    key = jax.random.fold_in(key, 2)
    values = jnp.clip(jax.random.normal(jax.random.fold_in(key, 1), (ROLLOUTS, D), jnp.float32), -6.0, 6.0)
    return values.astype(jnp.bfloat16)


def draw_offsets(key, part):
    base, spread = shared_table(key)
    key = jax.random.fold_in(key, 3)
    values = jnp.clip(jax.random.normal(jax.random.fold_in(key, 1), (ROLLOUTS, D), jnp.float32), -4.0, 4.0) * (0.5 * spread)
    return values.astype(jnp.bfloat16)


def plant(array, key, least, high):
    longest = array.shape.index(max(array.shape))
    spots = []
    for shift in (0, 1):
        where = [jax.random.randint(jax.random.fold_in(key, axis), (), 0, length) for axis, length in enumerate(array.shape)]
        where[longest] = (where[longest] + shift) % array.shape[longest]
        spots.append(tuple(where))
    return array.at[spots[0]].set(least).at[spots[1]].set(high)


def setup_inputs(seed: int = 0) -> dict:
    keys = jax.random.split(jax.random.key(seed), 8)
    return {
        "start_hidden": draw_start_hidden(jax.random.fold_in(keys[7], 71), 0),
        "offsets": draw_offsets(jax.random.fold_in(keys[7], 71), 0),
        "norm_gain": jnp.clip(1.0 + 0.1 * jax.random.normal(keys[2], (D,), jnp.float32), 0.5, 1.5),
        "head_table": draw_head_table(jax.random.fold_in(keys[7], 71), 0),
        "targets_one": plant(jax.random.randint(keys[4], (ROLLOUTS,), 0, VOCAB), jax.random.fold_in(keys[4], 1), 0, VOCAB - 1).astype(jnp.int32),
        "targets_two": plant(jax.random.randint(keys[5], (ROLLOUTS,), 0, VOCAB), jax.random.fold_in(keys[5], 1), 0, VOCAB - 1).astype(jnp.int32),
        "advantage": plant(jax.random.randint(keys[6], (ROLLOUTS,), -2, 3), jax.random.fold_in(keys[6], 1), -2, 2).astype(jnp.int32),
    }


ENTROPY_WEIGHT = 0.05
NORM_EPS = 1e-05

def head_softmax(inputs, head_table):
    logits = jnp.dot(inputs, head_table.T, preferred_element_type=jnp.float32)
    row_top = lax.optimization_barrier(jnp.max(logits, axis=1, keepdims=True))
    expo = jnp.exp(logits - row_top)
    total = lax.optimization_barrier(jnp.sum(expo, axis=1, keepdims=True))
    weighted = lax.optimization_barrier(jnp.sum(expo * logits, axis=1, keepdims=True))
    log_total = row_top + jnp.log(total)
    probs = jnp.exp(logits - log_total)
    return (logits, probs, weighted / total)

def logit_grad(logits, probs, mean_logit, targets, advantage_f):
    columns = jnp.arange(logits.shape[1], dtype=jnp.int32)
    onehot = (columns[None, :] == targets[:, None]).astype(jnp.float32)
    return -advantage_f * (onehot - probs) + ENTROPY_WEIGHT * probs * (logits - mean_logit)

def contract_rows(left, right):
    return lax.dot_general(left, right, (((0,), (0,)), ((), ())), preferred_element_type=jnp.float32)

def reference(start_hidden, offsets, norm_gain, head_table, targets_one, targets_two, advantage):
    advantage_f = advantage.astype(jnp.float32)[:, None]
    logits_one, probs_one, mean_one = head_softmax(start_hidden, head_table)
    probs_low = probs_one.astype(jnp.bfloat16)
    mixed = jnp.dot(probs_low, head_table, preferred_element_type=jnp.float32)
    state = mixed + offsets.astype(jnp.float32)
    rms = jnp.sqrt(lax.optimization_barrier(jnp.mean(state * state, axis=1, keepdims=True)) + NORM_EPS)
    unit = state / rms
    next_input = (unit * norm_gain[None, :]).astype(jnp.bfloat16)
    logits_two, probs_two, mean_two = head_softmax(next_input, head_table)
    grad_two = logit_grad(logits_two, probs_two, mean_two, targets_two, advantage_f).astype(jnp.bfloat16)
    input_grad = jnp.dot(grad_two, head_table, preferred_element_type=jnp.float32)
    gain_grad = lax.optimization_barrier(jnp.sum(input_grad * unit, axis=0))
    scaled = input_grad * norm_gain[None, :]
    offset_grad = ((scaled - unit * lax.optimization_barrier(jnp.mean(scaled * unit, axis=1, keepdims=True))) / rms).astype(jnp.bfloat16)
    prob_grad = jnp.dot(offset_grad, head_table.T, preferred_element_type=jnp.float32)
    inner = lax.optimization_barrier(jnp.sum(probs_low.astype(jnp.float32) * prob_grad, axis=1, keepdims=True))
    grad_one = logit_grad(logits_one, probs_one, mean_one, targets_one, advantage_f) + probs_one * (prob_grad - inner)
    grad_one = grad_one.astype(jnp.bfloat16)
    head_grad = contract_rows(grad_one, start_hidden) + contract_rows(probs_low, offset_grad) + contract_rows(grad_two, next_input)
    return (head_grad, gain_grad, offset_grad)
```

```python
import jax
import jax.numpy as jnp
from jax import lax
from jax.sharding import Mesh, PartitionSpec as P

ENTROPY_WEIGHT = 0.05
NORM_EPS = 1e-05
DP = ("zh", "y")
VOCAB = ("x", "zl", "c")
CHIPS = ("zh", "y", "x", "zl")
SWAP = [(0, 1), (1, 0)]
f32 = jnp.float32
bf16 = jnp.bfloat16


def mm(left, right):
    return lax.dot_general(left, right, (((1,), (0,)), ((), ())), preferred_element_type=f32)


def mm_nt(left, right):
    return lax.dot_general(left, right, (((1,), (1,)), ((), ())), preferred_element_type=f32)


def mm_tn(left, right):
    return lax.dot_general(left, right, (((0,), (0,)), ((), ())), preferred_element_type=f32)


def swap(value):
    return lax.ppermute(value, "c", SWAP)


def exchange(blocks, axes):
    return lax.all_to_all(blocks, axes, 0, 0)


def spread(piece, axes):
    n = lax.axis_size(axes)
    return exchange(jnp.broadcast_to(piece[None], (n,) + piece.shape), axes)


def local(start_hidden, offsets, norm_gain, head_table, targets_one, targets_two, advantage):
    core = lax.axis_index("c")
    chip = lax.axis_index(CHIPS)
    sub = lax.axis_index(("x", "zl"))
    n_dp = lax.axis_size(DP)
    n_chip = lax.axis_size(CHIPS)
    own_rows, width = start_hidden.shape
    half = own_rows // 2
    rows = n_dp * half
    piece = rows // n_chip
    block_rows = head_table.shape[0]

    def core_rows(values):
        grouped = values.reshape(n_dp, 2, half)
        return lax.dynamic_slice_in_dim(grouped, core, 1, 1).reshape(rows)

    first = (lax.axis_index(DP) * lax.axis_size(VOCAB) + lax.axis_index(VOCAB)) * block_rows
    other_first = first + (1 - 2 * core) * block_rows
    columns = (
        first + lax.iota(jnp.int32, block_rows),
        other_first + lax.iota(jnp.int32, block_rows),
    )
    tg_one = core_rows(targets_one)
    tg_two = core_rows(targets_two)
    adv = core_rows(advantage).astype(f32)[:, None]
    gain = norm_gain[None, :]

    tables = (head_table, swap(head_table))

    def logit_grad(logits, probs, mean_logit, targets, cols):
        onehot = (cols[None, :] == targets[:, None]).astype(f32)
        return -adv * (onehot - probs) + ENTROPY_WEIGHT * probs * (logits - mean_logit)

    def local_stats(logits):
        top = jnp.maximum(jnp.max(logits[0], axis=1), jnp.max(logits[1], axis=1))
        shifted = [l - top[:, None] for l in logits]
        expo = [jnp.exp(s) for s in shifted]
        total = jnp.sum(expo[0], axis=1) + jnp.sum(expo[1], axis=1)
        weighted = jnp.sum(expo[0] * shifted[0], axis=1) + jnp.sum(expo[1] * shifted[1], axis=1)
        return top, total, weighted

    def all_stats(top, total, weighted):
        packed = jnp.concatenate([top, total, weighted, jnp.zeros((1024 - 3 * rows,), f32)])
        stats = spread(packed.reshape(8, 128), CHIPS).reshape(n_chip, 1024)
        top, total, weighted = (stats[:, k * rows : (k + 1) * rows] for k in range(3))
        peak = jnp.max(top, axis=0)
        scale = jnp.exp(top - peak[None])
        total_all = jnp.sum(scale * total, axis=0)
        weighted_all = jnp.sum(scale * (weighted + (top - peak[None]) * total), axis=0)
        lse = peak + jnp.log(total_all)
        return lse[:, None], (peak + weighted_all / total_all)[:, None]

    own_half = lax.dynamic_slice_in_dim(start_hidden, core * half, half, 0)
    hidden = spread(own_half, DP).reshape(rows, width)
    hidden_other = swap(hidden)
    logits_one = [mm_nt(hidden, t) for t in tables]
    lse_one, mean_one = all_stats(*local_stats(logits_one))
    probs_one = [jnp.exp(l - lse_one) for l in logits_one]
    probs_low = [p.astype(bf16) for p in probs_one]
    partial = (mm(probs_low[0], tables[0]) + mm(probs_low[1], tables[1])).astype(bf16)
    parts = exchange(partial.reshape(n_chip, piece, width), CHIPS)
    mixed = jnp.sum(parts.astype(f32), axis=0)
    own_offsets = lax.dynamic_slice_in_dim(offsets, core * half + sub * piece, piece, 0).astype(f32)
    state = mixed + own_offsets
    rms = jnp.sqrt(jnp.mean(state * state, axis=1, keepdims=True) + NORM_EPS)
    unit = state / rms
    next_piece = (unit * gain).astype(bf16)
    next_input = spread(next_piece, CHIPS).reshape(rows, width)
    next_other = swap(next_input)

    logits_two = [mm_nt(next_input, t) for t in tables]
    lse_two, mean_two = all_stats(*local_stats(logits_two))
    grad_two = [
        logit_grad(l, jnp.exp(l - lse_two), mean_two, tg_two, c).astype(bf16)
        for l, c in zip(logits_two, columns)
    ]
    partial = (mm(grad_two[0], tables[0]) + mm(grad_two[1], tables[1])).astype(bf16)
    parts = exchange(partial.reshape(n_chip, piece, width), CHIPS)
    input_grad = jnp.sum(parts.astype(f32), axis=0)
    scaled = input_grad * gain
    offset_piece = (
        (scaled - unit * jnp.mean(scaled * unit, axis=1, keepdims=True)) / rms
    ).astype(bf16)
    offset_rows = spread(offset_piece, CHIPS).reshape(rows, width)
    offset_other = swap(offset_rows)

    share = width // n_chip
    gain_part = jnp.sum(input_grad * unit, axis=0).reshape(n_chip, 1, share)
    gain_part = exchange(jnp.pad(gain_part, ((0, 0), (0, 0), (0, 128 - share))), CHIPS)
    gain_sum = jnp.sum(gain_part, axis=0)[0, :share]
    inner_piece = jnp.sum(offset_piece.astype(f32) * mixed, axis=1)
    packed = jnp.concatenate([gain_sum, inner_piece, jnp.zeros((128 - share - piece,), f32)])
    packed = spread(packed.reshape(1, 128), CHIPS)[:, 0]
    gain_half = packed[:, :share].reshape(width)
    inner = packed[:, share : share + piece].reshape(rows, 1)
    gain_grad = gain_half + swap(gain_half)

    low_other = swap(probs_low[1])
    two_other = swap(grad_two[1])
    grad_one = [
        (logit_grad(l, p, mean_one, tg_one, c) + p * (mm_nt(offset_rows, t) - inner)).astype(bf16)
        for l, p, c, t in zip(logits_one, probs_one, columns, tables)
    ]
    one_other = swap(grad_one[1])
    head_grad = mm_tn(grad_two[0], next_input) + mm_tn(two_other, next_other)
    head_grad = head_grad + mm_tn(probs_low[0], offset_rows) + mm_tn(low_other, offset_other)
    head_grad = head_grad + mm_tn(grad_one[0], hidden) + mm_tn(one_other, hidden_other)

    dp = lax.axis_index(DP)
    mine = lax.dynamic_slice_in_dim(offset_rows, dp * half, half, 0)
    theirs = lax.dynamic_slice_in_dim(offset_other, dp * half, half, 0)
    lower = jnp.where(core == 0, mine, theirs)
    upper = jnp.where(core == 0, theirs, mine)
    offset_grad = jnp.concatenate([lower, upper], axis=0)
    return (head_grad, gain_grad, offset_grad)


def solution(mesh):
    fine = Mesh(mesh.devices.reshape(2, 4, 4, 2, 2), ("zh", "y", "x", "zl", "c"))
    rows = DP + VOCAB
    return jax.shard_map(
        local,
        mesh=fine,
        in_specs=(P(DP, None), P(DP, None), P(), P(rows, None), P(), P(), P()),
        out_specs=(P(rows, None), P(), P(DP, None)),
        check_vma=False,
    )
```

```python
import functools

import jax
import jax.numpy as jnp
from jax import lax
from jax.experimental import pallas as pl
from jax.experimental.pallas import tpu as pltpu
from jax.sharding import Mesh, PartitionSpec as P

ENTROPY_WEIGHT = 0.05
NORM_EPS = 1e-05
DP = ("zh", "y")
VOCAB = ("x", "zl", "c")
CHIPS = ("zh", "y", "x", "zl")
SWAP = [(0, 1), (1, 0)]
VOCAB_TILE = 256
WIDTH_TILE = 512
LANES = 128
f32 = jnp.float32
bf16 = jnp.bfloat16
PARAMS = pltpu.CompilerParams(vmem_limit_bytes=56 * 1024 * 1024)


def swap(value):
    return lax.ppermute(value, "c", SWAP)


def exchange(blocks, axes):
    return lax.all_to_all(blocks, axes, 0, 0)


def spread(piece, axes):
    n = lax.axis_size(axes)
    return exchange(jnp.broadcast_to(piece[None], (n,) + piece.shape), axes)


def thirds(value):
    high = lax.reduce_precision(value, 8, 7)
    middle = lax.reduce_precision(value - high, 8, 7)
    return [v.astype(bf16) for v in (high, middle, value - high - middle)]


def full(shape):
    return pl.BlockSpec(shape, lambda *_: (0,) * len(shape))


def gather_rows(pieces_ref, rows_ref):
    width = rows_ref.shape[1]
    for j in range(rows_ref.shape[0] // 16):
        part = [pieces_ref[4 * j + k, :, :width].astype(f32) for k in range(4)]
        rows_ref[16 * j : 16 * j + 16, :] = jnp.concatenate(part, axis=0).astype(bf16)


def scatter_rows(value, pieces_ref, start):
    for j in range(value.shape[0] // 4):
        pieces_ref[j, :, pl.ds(start, value.shape[1])] = value[4 * j : 4 * j + 4].astype(bf16)


def nt(left, right):
    return lax.dot_general(left, right, (((1,), (1,)), ((), ())), preferred_element_type=f32)


def logits_kernel(steps, assemble, *refs):
    if assemble:
        pieces, own, other, logits, stats, hidden = refs
    else:
        hidden, own, other, logits, stats = refs
    i = pl.program_id(0)

    @pl.when(i == 0)
    def _():
        if assemble:
            gather_rows(pieces, hidden)
        stats[...] = jnp.zeros_like(stats)
        stats[0:1, :] = jnp.full((1, stats.shape[1]), -1e30, f32)

    def step(table):
        tile = nt(table[...], hidden[...])
        logits[...] = tile
        old, total, weighted = stats[0:1, :], stats[1:2, :], stats[2:3, :]
        top = jnp.maximum(old, jnp.max(tile, axis=0, keepdims=True))
        shifted = tile - top
        expo = jnp.exp(shifted)
        scale = jnp.exp(old - top)
        stats[0:1, :] = top
        stats[1:2, :] = scale * total + jnp.sum(expo, axis=0, keepdims=True)
        stats[2:3, :] = scale * (weighted + (old - top) * total) + jnp.sum(
            expo * shifted, axis=0, keepdims=True
        )

    @pl.when(i < steps)
    def _():
        step(own)

    @pl.when(i >= steps)
    def _():
        step(other)


def logits_call(hidden, tables):
    block, width = tables[0].shape
    assemble = hidden.ndim == 3
    rows = hidden.size // width
    steps = block // VOCAB_TILE
    out_shape = [
        jax.ShapeDtypeStruct((2 * block, rows), f32),
        jax.ShapeDtypeStruct((8, rows), f32),
    ]
    out_specs = [pl.BlockSpec((VOCAB_TILE, rows), lambda i: (i, 0)), full((8, rows))]
    if assemble:
        out_shape.append(jax.ShapeDtypeStruct((rows, width), bf16))
        out_specs.append(full((rows, width)))
    return pl.pallas_call(
        functools.partial(logits_kernel, steps, assemble),
        grid=(2 * steps,),
        in_specs=[
            full(hidden.shape),
            pl.BlockSpec((VOCAB_TILE, width), lambda i: (jnp.minimum(i, steps - 1), 0)),
            pl.BlockSpec((VOCAB_TILE, width), lambda i: (jnp.maximum(i - steps, 0), 0)),
        ],
        out_shape=out_shape,
        out_specs=out_specs,
        compiler_params=PARAMS,
    )(hidden, *tables)


def row_values(rows):
    return rows[0:1, :], rows[1:2, :], rows[2:3, :], rows[3:4, :]


def logit_grad(logits, probs, rows, entries, targets):
    _, mean, adv, _ = row_values(rows)
    onehot = (entries == targets[0:1, :]).astype(f32)
    return -adv * (onehot - probs) + ENTROPY_WEIGHT * probs * (logits - mean)


def entries_of(first, n, rows):
    return first + lax.broadcasted_iota(jnp.int32, (n, rows), 0)


def mixture_kernel(with_grad, *refs):
    if with_grad:
        first, logits, rows, targets, own, other, hidden, gain, coef, partial, turned = refs
    else:
        logits, rows, own, other, coef, partial, turned = refs
    i = pl.program_id(0)
    block = own.shape[0]
    width_tile = own.shape[1]
    n_rows = logits.shape[1]

    @pl.when(i == 0)
    def _():
        for j in range(0, 2 * block, VOCAB_TILE):
            tile = logits[j : j + VOCAB_TILE, :]
            probs = jnp.exp(tile - rows[0:1, :])
            if with_grad:
                start = first[j // block] + j % block
                entries = entries_of(start, VOCAB_TILE, n_rows)
                probs = logit_grad(tile, probs, rows, entries, targets)
            coef[j : j + VOCAB_TILE, :] = probs.astype(bf16)
            turned[:, j : j + VOCAB_TILE] = probs.T.astype(bf16)
        if with_grad:
            partial[:, :, partial.shape[2] - LANES :] = jnp.zeros(
                (partial.shape[0], 4, LANES), bf16
            )

    value = jnp.dot(turned[:, :block], own[...], preferred_element_type=f32)
    value = value + jnp.dot(turned[:, block:], other[...], preferred_element_type=f32)
    scatter_rows(value, partial, pl.multiple_of(i * width_tile, width_tile))
    if with_grad:
        unit = hidden[...].astype(f32) / gain[...]
        share = jnp.sum(unit * value, axis=0, keepdims=True)
        high = share.astype(bf16).astype(f32)
        middle = (share - high).astype(bf16).astype(f32)
        low = share - high - middle
        parts = jnp.concatenate([high, middle, low, jnp.zeros_like(low)], axis=0).astype(bf16)
        last = partial.shape[2] - LANES
        for k in range(width_tile // LANES):
            partial[i * (width_tile // LANES) + k, :, last:] = parts[:, k * LANES : (k + 1) * LANES]


def mixture_call(logits, rows, tables, grad=None):
    block, width = tables[0].shape
    n_rows = logits.shape[1]
    pieces = n_rows // 4
    table_spec = pl.BlockSpec((block, WIDTH_TILE), lambda i: (0, i))
    in_specs = [full(logits.shape), full(rows.shape), table_spec, table_spec]
    operands = [logits, rows, *tables]
    out_width = width
    if grad is not None:
        first, targets, hidden, gain = grad
        out_width += LANES
        in_specs[2:2] = [full(targets.shape)]
        in_specs = [pl.BlockSpec(memory_space=pltpu.SMEM)] + in_specs
        in_specs += [
            pl.BlockSpec((n_rows, WIDTH_TILE), lambda i: (0, i)),
            pl.BlockSpec((1, WIDTH_TILE), lambda i: (0, i)),
        ]
        operands = [first, logits, rows, targets, *tables, hidden, gain]
    return pl.pallas_call(
        functools.partial(mixture_kernel, grad is not None),
        grid=(width // WIDTH_TILE,),
        in_specs=in_specs,
        out_shape=[
            jax.ShapeDtypeStruct((2 * block, n_rows), bf16),
            jax.ShapeDtypeStruct((pieces, 4, out_width), bf16),
        ],
        out_specs=[full((2 * block, n_rows)), full((pieces, 4, out_width))],
        scratch_shapes=[pltpu.VMEM((n_rows, 2 * block), bf16)],
        compiler_params=PARAMS,
    )(*operands)


def first_grad_kernel(assemble, *refs):
    if assemble:
        first, pieces, logits, rows, targets, table, grad, hidden = refs
    else:
        first, hidden, logits, rows, targets, table, grad = refs
    i = pl.program_id(0)
    if assemble:

        @pl.when(i == 0)
        def _():
            gather_rows(pieces, hidden)

    prob_grad = nt(table[...], hidden[...])
    tile = logits[...]
    lse, _, _, inner = row_values(rows)
    probs = jnp.exp(tile - lse)
    entries = entries_of(first[0] + i * tile.shape[0], *tile.shape)
    value = logit_grad(tile, probs, rows, entries, targets) + probs * (prob_grad - inner)
    grad[...] = value.astype(bf16)


def first_grad_call(hidden, logits, half, rows, targets, table, first):
    block, width = table.shape
    assemble = hidden.ndim == 3
    n_rows = logits.shape[1]
    steps = block // VOCAB_TILE
    out_shape = [jax.ShapeDtypeStruct((block, n_rows), bf16)]
    out_specs = [pl.BlockSpec((VOCAB_TILE, n_rows), lambda i: (i, 0))]
    if assemble:
        out_shape.append(jax.ShapeDtypeStruct((n_rows, width), bf16))
        out_specs.append(full((n_rows, width)))
    return pl.pallas_call(
        functools.partial(first_grad_kernel, assemble),
        grid=(steps,),
        in_specs=[
            pl.BlockSpec(memory_space=pltpu.SMEM),
            full(hidden.shape),
            pl.BlockSpec((VOCAB_TILE, n_rows), lambda i: (half * steps + i, 0)),
            full(rows.shape),
            full(targets.shape),
            pl.BlockSpec((VOCAB_TILE, width), lambda i: (i, 0)),
        ],
        out_shape=out_shape,
        out_specs=out_specs,
        compiler_params=PARAMS,
    )(first, hidden, logits, rows, targets, table)


def head_kernel(*refs):
    n = len(refs) // 2
    left = jnp.concatenate([r[...] for r in refs[:n]], axis=1)
    right = jnp.concatenate([r[...] for r in refs[n : 2 * n]], axis=0)
    refs[-1][...] = jnp.dot(left, right, preferred_element_type=f32)


def head_call(pairs, block):
    n_rows, width = pairs[0][1].shape
    return pl.pallas_call(
        head_kernel,
        grid=(width // WIDTH_TILE,),
        in_specs=[full((block, n_rows))] * len(pairs)
        + [pl.BlockSpec((n_rows, WIDTH_TILE), lambda i: (0, i))] * len(pairs),
        out_shape=jax.ShapeDtypeStruct((block, width), f32),
        out_specs=pl.BlockSpec((block, WIDTH_TILE), lambda i: (0, i)),
        compiler_params=PARAMS,
    )(*[p[0] for p in pairs], *[p[1] for p in pairs])


def local(start_hidden, offsets, norm_gain, head_table, targets_one, targets_two, advantage):
    core = lax.axis_index("c")
    sub = lax.axis_index(("x", "zl"))
    n_dp = lax.axis_size(DP)
    n_chip = lax.axis_size(CHIPS)
    own_rows, width = start_hidden.shape
    half = own_rows // 2
    rows = n_dp * half
    piece = rows // n_chip
    block_rows = head_table.shape[0]
    owners = width // LANES

    def core_rows(values):
        grouped = values.reshape(n_dp, 2, half)
        return lax.dynamic_slice_in_dim(grouped, core, 1, 1).reshape(1, rows)

    first = (lax.axis_index(DP) * lax.axis_size(VOCAB) + lax.axis_index(VOCAB)) * block_rows
    first = jnp.stack([first, first + (1 - 2 * core) * block_rows])
    tg_one = core_rows(targets_one)
    tg_two = core_rows(targets_two)
    adv = core_rows(advantage).astype(f32)
    gain = norm_gain[None, :]
    tables = (head_table, swap(head_table))

    def all_stats(stats):
        packed = stats[:4].reshape(8 * rows // 256, 128)
        stats = spread(packed, CHIPS).reshape(n_chip, 4, rows)
        top, total, weighted = stats[:, 0], stats[:, 1], stats[:, 2]
        peak = jnp.max(top, axis=0)
        scale = jnp.exp(top - peak[None])
        total_all = jnp.sum(scale * total, axis=0)
        weighted_all = jnp.sum(scale * (weighted + (top - peak[None]) * total), axis=0)
        lse = peak + jnp.log(total_all)
        return lse[None], (peak + weighted_all / total_all)[None]

    own_half = lax.dynamic_slice_in_dim(start_hidden, core * half, half, 0)
    hidden = spread(own_half, DP).reshape(rows, width)
    hidden_other = swap(hidden)
    logits_one, stats = logits_call(hidden, tables)
    lse_one, mean_one = all_stats(stats)
    low, partial = mixture_call(logits_one, lse_one, tables)
    parts = exchange(partial, CHIPS)
    mixed = jnp.sum(parts.astype(f32), axis=0)
    own_offsets = lax.dynamic_slice_in_dim(offsets, core * half + sub * piece, piece, 0).astype(f32)
    state = mixed + own_offsets
    rms = jnp.sqrt(jnp.mean(state * state, axis=1, keepdims=True) + NORM_EPS)
    unit = state / rms
    next_piece = (unit * gain).astype(bf16)
    next_pieces = spread(next_piece, CHIPS)

    logits_two, stats, next_input = logits_call(next_pieces, tables)
    next_other = swap(next_input)
    lse_two, mean_two = all_stats(stats)
    rows_two = jnp.concatenate([lse_two, mean_two, adv, adv], axis=0)
    grad_two, partial = mixture_call(
        logits_two, rows_two, tables, (first, tg_two, next_input, gain)
    )
    parts = exchange(partial, CHIPS)
    sums = jnp.sum(parts.astype(f32), axis=0)
    input_grad = sums[:, :width]
    gain_share = sums[0, width:] + sums[1, width:] + sums[2, width:]
    scaled = input_grad * gain
    offset_piece = (
        (scaled - unit * jnp.mean(scaled * unit, axis=1, keepdims=True)) / rms
    ).astype(bf16)
    inner_piece = jnp.sum(offset_piece.astype(f32) * mixed, axis=1)
    inner_piece = jnp.concatenate(thirds(inner_piece) + [jnp.zeros((LANES - 3 * piece,), bf16)])
    extra = jnp.stack(thirds(gain_share) + [inner_piece])
    pieces = spread(jnp.concatenate([offset_piece, extra], axis=1), CHIPS)
    extra = pieces[:, :, width:].astype(f32)
    gain_half = jnp.sum(extra[:owners, :3], axis=1).reshape(width)
    gain_grad = gain_half + swap(gain_half)
    inner = extra[:, 3, : 3 * piece].reshape(n_chip, 3, piece).sum(axis=1).reshape(1, rows)

    low_other = swap(low[block_rows:])
    two_other = swap(grad_two[block_rows:])
    rows_one = jnp.concatenate([lse_one, mean_one, adv, inner], axis=0)
    grad_b, offset_rows = first_grad_call(
        pieces, logits_one, 1, rows_one, tg_one, tables[1], first[1:]
    )
    one_other = swap(grad_b)
    offset_other = swap(offset_rows)
    (grad_a,) = first_grad_call(offset_rows, logits_one, 0, rows_one, tg_one, tables[0], first[:1])
    head_grad = head_call(
        [
            (grad_two, next_input),
            (two_other, next_other),
            (low, offset_rows),
            (grad_a, hidden),
            (low_other, offset_other),
            (one_other, hidden_other),
        ],
        block_rows,
    )

    dp = lax.axis_index(DP)
    mine = lax.dynamic_slice_in_dim(offset_rows, dp * half, half, 0)
    theirs = lax.dynamic_slice_in_dim(offset_other, dp * half, half, 0)
    lower = jnp.where(core == 0, mine, theirs)
    upper = jnp.where(core == 0, theirs, mine)
    offset_grad = jnp.concatenate([lower, upper], axis=0)
    return (head_grad, gain_grad, offset_grad)


def solution(mesh):
    fine = Mesh(mesh.devices.reshape(2, 4, 4, 2, 2), ("zh", "y", "x", "zl", "c"))
    rows = DP + VOCAB
    return jax.shard_map(
        local,
        mesh=fine,
        in_specs=(P(DP, None), P(DP, None), P(), P(rows, None), P(), P(), P()),
        out_specs=(P(rows, None), P(), P(DP, None)),
        check_vma=False,
    )
```

```python
import functools

import jax
import jax.numpy as jnp
from jax import lax
from jax.experimental import pallas as pl
from jax.experimental.pallas import tpu as pltpu
from jax.sharding import Mesh, PartitionSpec as P

ENTROPY_WEIGHT = 0.05
NORM_EPS = 1e-05
DP = ("zh", "y")
VOCAB = ("x", "zl", "c")
CHIPS = ("zh", "y", "x", "zl")
SWAP = [(0, 1), (1, 0)]
VOCAB_TILE = 256
WIDTH_TILE = 512
LANES = 128
f32 = jnp.float32
bf16 = jnp.bfloat16


def swap(value):
    return lax.ppermute(value, "c", SWAP)


def exchange(blocks, axes):
    return lax.all_to_all(blocks, axes, 0, 0)


def spread(piece, axes):
    n = lax.axis_size(axes)
    return exchange(jnp.broadcast_to(piece[None], (n,) + piece.shape), axes)


def whole():
    return pl.BlockSpec(memory_space=pltpu.VMEM)


def in_vmem(value):
    return pltpu.with_memory_space_constraint(value, pltpu.VMEM)


def call(kernel, operands, out_shape, scratch_shapes=(), scalars=0, vmem=16, far=()):
    specs = [pl.BlockSpec(memory_space=pltpu.SMEM)] * scalars
    specs += [whole()] * (len(operands) - scalars)
    for k in far:
        specs[k] = pl.BlockSpec(memory_space=pl.ANY)
    return pl.pallas_call(
        kernel,
        in_specs=specs,
        out_shape=out_shape,
        out_specs=[whole()] * len(out_shape),
        scratch_shapes=scratch_shapes,
        compiler_params=pltpu.CompilerParams(vmem_limit_bytes=vmem * 1024 * 1024),
    )(*operands)


def gather_rows(pieces_ref, rows_ref):
    width = rows_ref.shape[1]
    for j in range(rows_ref.shape[0] // 16):
        part = [pieces_ref[4 * j + k, :, :width].astype(f32) for k in range(4)]
        rows_ref[16 * j : 16 * j + 16, :] = jnp.concatenate(part, axis=0).astype(bf16)


def scatter_rows(value, pieces_ref, start):
    for j in range(value.shape[0] // 4):
        pieces_ref[j, :, start : start + value.shape[1]] = value[4 * j : 4 * j + 4].astype(bf16)


def nt(left, right):
    return lax.dot_general(left, right, (((1,), (1,)), ((), ())), preferred_element_type=f32)


def together(*values):
    return lax.optimization_barrier(values)


def logits_kernel(second, *refs):
    if second:
        pieces, own, other, logits, stats, hidden = refs
        gather_rows(pieces, hidden)
    else:
        hidden, far_own, far_other, logits, stats, own, other, sems = refs
        steps = own.shape[0] // VOCAB_TILE
        copies = [
            pltpu.make_async_copy(
                far.at[pl.ds(k * VOCAB_TILE, VOCAB_TILE)],
                near.at[pl.ds(k * VOCAB_TILE, VOCAB_TILE)],
                sems.at[t * steps + k],
            )
            for t, (far, near) in enumerate(((far_own, own), (far_other, other)))
            for k in range(steps)
        ]
        for copy in copies:
            copy.start()
    n_rows = logits.shape[1]
    block = other.shape[0]
    old = jnp.full((1, n_rows), -1e30, f32)
    total = jnp.zeros((1, n_rows), f32)
    weighted = total
    for table, base in ((own, 0), (other, block)):
        for start in range(0, block, VOCAB_TILE):
            if not second:
                copies[(base + start) // VOCAB_TILE].wait()
            tile = nt(table[start : start + VOCAB_TILE, :], hidden[...])
            logits[base + start : base + start + VOCAB_TILE, :] = tile
            top = jnp.maximum(old, jnp.max(tile, axis=0, keepdims=True))
            shifted = tile - top
            expo = jnp.exp(shifted)
            scale = jnp.exp(old - top)
            weighted = scale * (weighted + (old - top) * total) + jnp.sum(
                expo * shifted, axis=0, keepdims=True
            )
            total = scale * total + jnp.sum(expo, axis=0, keepdims=True)
            old = top
    lines = [v[:, k : k + LANES] for v in (old, total, weighted) for k in range(0, n_rows, LANES)]
    lines += [jnp.zeros((1, LANES), f32)] * (stats.shape[1] - len(lines))
    stats[...] = jnp.broadcast_to(jnp.concatenate(lines, axis=0)[None], stats.shape)


def logits_call(hidden, tables, n_chip):
    block, width = tables[0].shape
    second = hidden.ndim == 3
    rows = hidden.size // width
    out_shape = [
        pltpu.VMEM((2 * block, rows), f32),
        jax.ShapeDtypeStruct((n_chip, 8, LANES), f32),
    ]
    if second:
        out_shape.append(jax.ShapeDtypeStruct((rows, width), bf16))
        return call(
            functools.partial(logits_kernel, True),
            [hidden, in_vmem(tables[0]), in_vmem(tables[1])],
            out_shape,
        )
    out_shape += [pltpu.VMEM((block, width), bf16)] * 2
    return call(
        functools.partial(logits_kernel, False),
        [hidden] + [pltpu.with_memory_space_constraint(t, pltpu.HBM) for t in tables],
        out_shape,
        [pltpu.SemaphoreType.DMA((2 * block // VOCAB_TILE,))],
        far=(1, 2),
    )


def all_stats(stats, n_rows):
    n = n_rows // LANES
    top, total, weighted = (
        jnp.concatenate([stats[:, k * n + j, :] for j in range(n)], axis=1) for k in range(3)
    )
    peak = jnp.max(top, axis=0, keepdims=True)
    gap = top - peak
    scale = jnp.exp(gap)
    total_all = jnp.sum(scale * total, axis=0, keepdims=True)
    weighted_all = jnp.sum(scale * (weighted + gap * total), axis=0, keepdims=True)
    return peak + jnp.log(total_all), peak + weighted_all / total_all


def logit_grad(logits, probs, mean, adv, entries, targets):
    onehot = (entries == targets).astype(f32)
    return -adv * (onehot - probs) + ENTROPY_WEIGHT * probs * (logits - mean)


def entries_of(first, n, rows):
    return first + lax.broadcasted_iota(jnp.int32, (n, rows), 0)


def mixture_kernel(with_grad, *refs):
    if with_grad:
        first, logits, stats, targets, adv, own, other, hidden, gain = refs[:9]
    else:
        logits, stats, own, other = refs[:4]
    coef, partial, rows, turned = refs[-4:]
    block, width = own.shape
    n_rows = logits.shape[1]
    lse, mean = all_stats(stats, n_rows)
    rows[...] = jnp.concatenate([lse, mean] + [jnp.zeros_like(lse)] * 6, axis=0)
    for start in range(0, 2 * block, VOCAB_TILE):
        tile = logits[start : start + VOCAB_TILE, :]
        probs = jnp.exp(tile - lse)
        if with_grad:
            entry = first[start // block] + start % block
            entries = entries_of(entry, VOCAB_TILE, n_rows)
            probs = logit_grad(tile, probs, mean, adv[...], entries, targets[...])
        coef[start : start + VOCAB_TILE, :] = probs.astype(bf16)
        turned[:, start : start + VOCAB_TILE] = probs.T.astype(bf16)
    if with_grad:
        filled = width // LANES
        partial[filled:, :, width:] = jnp.zeros((partial.shape[0] - filled, 4, LANES), bf16)
    for start in range(0, width, WIDTH_TILE):
        columns = slice(start, start + WIDTH_TILE)
        value = jnp.dot(turned[:, :block], own[:, columns], preferred_element_type=f32)
        value = value + jnp.dot(turned[:, block:], other[:, columns], preferred_element_type=f32)
        scatter_rows(value, partial, start)
        if with_grad:
            unit = hidden[:, columns].astype(f32) / gain[:, columns]
            share = jnp.sum(unit * value, axis=0, keepdims=True)
            high = share.astype(bf16).astype(f32)
            middle = (share - high).astype(bf16).astype(f32)
            low = share - high - middle
            parts = jnp.concatenate([high, middle, low, jnp.zeros_like(low)], axis=0).astype(bf16)
            for k in range(WIDTH_TILE // LANES):
                piece = start // LANES + k
                partial[piece, :, width:] = parts[:, k * LANES : (k + 1) * LANES]


def mixture_call(logits, stats, tables, grad=None):
    block, width = tables[0].shape
    n_rows = logits.shape[1]
    tables = [in_vmem(t) for t in tables]
    operands = [in_vmem(logits), stats, *tables]
    out_width = width
    scalars = 0
    if grad is not None:
        first, targets, adv, hidden, gain = grad
        out_width += LANES
        operands = [first, in_vmem(logits), stats, targets, adv, *tables, hidden, gain]
        scalars = 1
    return call(
        functools.partial(mixture_kernel, grad is not None),
        operands,
        [
            jax.ShapeDtypeStruct((2 * block, n_rows), bf16),
            jax.ShapeDtypeStruct((n_rows // 4, 4, out_width), bf16),
            jax.ShapeDtypeStruct((8, n_rows), f32),
        ],
        [pltpu.VMEM((n_rows, 2 * block), bf16)],
        scalars,
    )


def in_thirds(value):
    high = value.astype(bf16).astype(f32)
    middle = (value - high).astype(bf16).astype(f32)
    return high, middle, value - high - middle


def sum_pieces(parts):
    total = parts[0].astype(f32)
    for k in range(1, parts.shape[0]):
        total = total + parts[k].astype(f32)
    return total


def state_kernel(parts, offsets, gain, pieces, unit_out, mixed_out, rms_out):
    mixed = sum_pieces(parts)
    state = mixed + offsets[...]
    rms = jnp.sqrt(jnp.mean(state * state, axis=1, keepdims=True) + NORM_EPS)
    unit = state / rms
    unit_out[...] = unit
    mixed_out[...] = mixed
    rms_out[...] = jnp.broadcast_to(rms, rms_out.shape)
    value = (unit * gain[...]).astype(bf16)
    for k in range(pieces.shape[0]):
        pieces[k] = value


def state_call(parts, offsets, gain):
    piece, width = offsets.shape
    return call(
        state_kernel,
        [parts, offsets, gain],
        [
            jax.ShapeDtypeStruct(parts.shape, bf16),
            jax.ShapeDtypeStruct((piece, width), f32),
            jax.ShapeDtypeStruct((piece, width), f32),
            jax.ShapeDtypeStruct((piece, LANES), f32),
        ],
    )


def offset_kernel(parts, unit, mixed, rms, gain, pieces):
    sums = sum_pieces(parts)
    piece, width = unit.shape
    scaled = sums[:, :width] * gain[...]
    along = jnp.mean(scaled * unit[...], axis=1, keepdims=True)
    value = ((scaled - unit[...] * along) / rms[:, :1]).astype(bf16).astype(f32)
    inner = jnp.sum(value * mixed[...], axis=1, keepdims=True)
    share = sums[0:1, width:] + sums[1:2, width:] + sums[2:3, width:]
    share = jnp.concatenate(list(in_thirds(share)) + [jnp.zeros_like(share)], axis=0)
    lane = lax.broadcasted_iota(jnp.int32, (piece, LANES), 1)
    terms = jnp.zeros((piece, LANES), f32)
    for k, term in enumerate(in_thirds(inner)):
        terms = jnp.where(lane == k, term, terms)
    line = jnp.concatenate([value, share, terms], axis=1).astype(bf16)
    for k in range(pieces.shape[0]):
        pieces[k] = line


def offset_call(parts, unit, mixed, rms, gain):
    n, piece, _ = parts.shape
    return call(
        offset_kernel,
        [parts, unit, mixed, rms, gain],
        [jax.ShapeDtypeStruct((n, piece, unit.shape[1] + 2 * LANES), bf16)],
    )[0]


def first_grad_kernel(half, assemble, *refs):
    if assemble:
        first, pieces, logits, rows, targets, adv, table, grad, hidden, inner_out, gain = refs
        width = hidden.shape[1]
        gather_rows(pieces, hidden)
        terms = [pieces[k, :, width + LANES :].astype(f32) for k in range(pieces.shape[0])]
        terms = jnp.concatenate(terms, axis=0).T
        inner = terms[0:1, :] + terms[1:2, :] + terms[2:3, :]
        inner_out[...] = jnp.broadcast_to(inner, inner_out.shape)
        for k in range(gain.shape[0]):
            share = pieces[k, :, width : width + LANES].astype(f32)
            gain[k : k + 1, :] = share[0:1] + share[1:2] + share[2:3]
    else:
        first, hidden, logits, rows, targets, adv, table, inner_in, grad = refs
        inner = inner_in[0:1, :]
    block = table.shape[0]
    lse, mean = rows[0:1, :], rows[1:2, :]
    for start in range(0, block, VOCAB_TILE):
        prob_grad = nt(table[start : start + VOCAB_TILE, :], hidden[...])
        tile = logits[half * block + start : half * block + start + VOCAB_TILE, :]
        probs = jnp.exp(tile - lse)
        entries = entries_of(first[half] + start, *tile.shape)
        value = logit_grad(tile, probs, mean, adv[...], entries, targets[...])
        value = value + probs * (prob_grad - inner)
        grad[start : start + VOCAB_TILE, :] = value.astype(bf16)


def first_grad_call(hidden, logits, half, rows, targets, adv, table, first, inner=None):
    block, width = table.shape
    n_rows = logits.shape[1]
    out_shape = [jax.ShapeDtypeStruct((block, n_rows), bf16)]
    operands = [first, hidden, in_vmem(logits), rows, targets, adv, in_vmem(table)]
    if inner is None:
        out_shape += [
            jax.ShapeDtypeStruct((n_rows, width), bf16),
            jax.ShapeDtypeStruct((8, n_rows), f32),
            jax.ShapeDtypeStruct((width // LANES, LANES), f32),
        ]
    else:
        operands.append(inner)
    return call(
        functools.partial(first_grad_kernel, half, inner is None), operands, out_shape, (), 1
    )


def head_kernel(n, place, *refs):
    lefts, rights = refs[:n], refs[n : 2 * n]
    mine, theirs, gain_a, gain_b, head, offset, gain = refs[2 * n :]
    block = head.shape[0]
    half = offset.shape[0] // 2

    @pl.when(pl.program_id(0) == 0)
    def _():
        gain[...] = gain_a[...] + gain_b[...]
        at = pl.ds(pl.multiple_of(place[0] * half, half), half)
        low = place[1] == 0
        offset[:half, :] = jnp.where(low, mine[at, :], theirs[at, :])
        offset[half:, :] = jnp.where(low, theirs[at, :], mine[at, :])

    start = pl.multiple_of(pl.program_id(0) * WIDTH_TILE, WIDTH_TILE)
    left = jnp.concatenate([r[:block, :] for r in lefts], axis=1)
    right = jnp.concatenate([r[:, pl.ds(start, WIDTH_TILE)] for r in rights], axis=0)
    head[...] = jnp.dot(left, right, preferred_element_type=f32)


def head_call(pairs, block, place, offset_rows, offset_other, gain_a, gain_b, own_rows):
    width = pairs[0][1].shape[1]
    operands = [p[0] for p in pairs] + [p[1] for p in pairs]
    operands += [offset_rows, offset_other, gain_a, gain_b]
    return pl.pallas_call(
        functools.partial(head_kernel, len(pairs)),
        grid=(width // WIDTH_TILE,),
        in_specs=[pl.BlockSpec(memory_space=pltpu.SMEM)] + [whole()] * len(operands),
        out_shape=[
            jax.ShapeDtypeStruct((block, width), f32),
            jax.ShapeDtypeStruct((own_rows, width), bf16),
            jax.ShapeDtypeStruct(gain_a.shape, f32),
        ],
        out_specs=[pl.BlockSpec((block, WIDTH_TILE), lambda i: (0, i)), whole(), whole()],
        compiler_params=pltpu.CompilerParams(vmem_limit_bytes=24 * 1024 * 1024),
    )(place, *operands)


def local(start_hidden, offsets, norm_gain, head_table, targets_one, targets_two, advantage):
    core = lax.axis_index("c")
    sub = lax.axis_index(("x", "zl"))
    n_dp = lax.axis_size(DP)
    n_chip = lax.axis_size(CHIPS)
    own_rows, width = start_hidden.shape
    half = own_rows // 2
    rows = n_dp * half
    piece = rows // n_chip
    block_rows = head_table.shape[0]

    def core_rows(values):
        grouped = values.reshape(n_dp, 2, half)
        return lax.dynamic_slice_in_dim(grouped, core, 1, 1).reshape(1, rows)

    first = (lax.axis_index(DP) * lax.axis_size(VOCAB) + lax.axis_index(VOCAB)) * block_rows
    first = jnp.stack([first, first + (1 - 2 * core) * block_rows])
    tg_one = core_rows(targets_one)
    tg_two = core_rows(targets_two)
    adv = core_rows(advantage).astype(f32)
    gain = norm_gain[None, :]
    own_offsets = lax.dynamic_slice_in_dim(offsets, core * half + sub * piece, piece, 0).astype(f32)
    place = jnp.stack([lax.axis_index(DP), core])
    tables = (head_table, swap(head_table))

    own_half = lax.dynamic_slice_in_dim(start_hidden, core * half, half, 0)
    hidden = spread(own_half, DP).reshape(rows, width)
    hidden, first, tg_one, tg_two, adv, gain, own_offsets, place = together(
        hidden, first, tg_one, tg_two, adv, gain, own_offsets, place
    )
    hidden_other = swap(hidden)
    logits_one, stats, *tables = logits_call(hidden, tables, n_chip)
    stats, hidden_other = together(stats, hidden_other)
    low, partial, rows_one = mixture_call(logits_one, exchange(stats, CHIPS), tables)
    pieces, unit, mixed, rms = state_call(exchange(partial, CHIPS), own_offsets, gain)

    pieces, low = together(exchange(pieces, CHIPS), low)
    low_other = swap(low[block_rows:])
    logits_two, stats, next_input = logits_call(pieces, tables, n_chip)
    stats, low_other = together(stats, low_other)
    stats, next_input = together(exchange(stats, CHIPS), next_input)
    next_other = swap(next_input)
    grad_two, partial, _ = mixture_call(
        logits_two, stats, tables, (first, tg_two, adv, next_input, gain)
    )
    partial, next_other = together(partial, next_other)
    pieces = offset_call(exchange(partial, CHIPS), unit, mixed, rms, gain)
    pieces, grad_two = together(exchange(pieces, CHIPS), grad_two)
    two_other = swap(grad_two[block_rows:])

    grad_b, offset_rows, inner, gain_half = first_grad_call(
        pieces, logits_one, 1, rows_one, tg_one, adv, tables[1], first
    )
    one_other = swap(grad_b)
    offset_other = swap(offset_rows)
    (grad_a,) = first_grad_call(
        offset_rows, logits_one, 0, rows_one, tg_one, adv, tables[0], first, inner
    )
    head_grad, offset_grad, gain_grad = head_call(
        [
            (grad_two, next_input),
            (two_other, next_other),
            (low, offset_rows),
            (grad_a, hidden),
            (low_other, offset_other),
            (one_other, hidden_other),
        ],
        block_rows,
        place,
        offset_rows,
        offset_other,
        gain_half,
        swap(gain_half),
        own_rows,
    )
    return (head_grad, gain_grad.reshape(width), offset_grad)


def solution(mesh):
    fine = Mesh(mesh.devices.reshape(2, 4, 4, 2, 2), ("zh", "y", "x", "zl", "c"))
    rows = DP + VOCAB
    return jax.shard_map(
        local,
        mesh=fine,
        in_specs=(P(DP, None), P(DP, None), P(), P(rows, None), P(), P(), P()),
        out_specs=(P(rows, None), P(), P(DP, None)),
        check_vma=False,
    )
```

```python
import functools

import jax
import jax.numpy as jnp
from jax import lax
from jax.experimental import pallas as pl
from jax.experimental.pallas import tpu as pltpu
from jax.sharding import Mesh, PartitionSpec as P

ENTROPY_WEIGHT = 0.05
NORM_EPS = 1e-05
DP = ("zh", "y")
VOCAB = ("x", "zl", "c")
CHIPS = ("zh", "y", "x", "zl")
SWAP = [(0, 1), (1, 0)]
VOCAB_TILE = 256
WIDTH_TILE = 512
HEAD_TILE = 256
LANES = 128
f32 = jnp.float32
bf16 = jnp.bfloat16


def swap(value):
    return lax.ppermute(value, "c", SWAP)


def exchange(blocks, axes):
    return lax.all_to_all(blocks, axes, 0, 0)


def whole():
    return pl.BlockSpec(memory_space=pltpu.VMEM)


def in_vmem(value):
    return pltpu.with_memory_space_constraint(value, pltpu.VMEM)


def call(kernel, operands, out_shape, scratch_shapes=(), scalars=0, vmem=16, far=()):
    specs = [pl.BlockSpec(memory_space=pltpu.SMEM)] * scalars
    specs += [whole()] * (len(operands) - scalars)
    for k in far:
        specs[k] = pl.BlockSpec(memory_space=pl.ANY)
    return pl.pallas_call(
        kernel,
        in_specs=specs,
        out_shape=out_shape,
        out_specs=[whole()] * len(out_shape),
        scratch_shapes=scratch_shapes,
        compiler_params=pltpu.CompilerParams(vmem_limit_bytes=vmem * 1024 * 1024),
    )(*operands)


def gather_rows(pieces_ref, rows_ref):
    width = rows_ref.shape[1]
    for j in range(rows_ref.shape[0] // 16):
        part = [pieces_ref[4 * j + k, :, :width].astype(f32) for k in range(4)]
        rows_ref[16 * j : 16 * j + 16, :] = jnp.concatenate(part, axis=0).astype(bf16)


def scatter_rows(value, pieces_ref, start):
    for j in range(value.shape[0] // 4):
        pieces_ref[j, :, start : start + value.shape[1]] = value[4 * j : 4 * j + 4].astype(bf16)


def nt(left, right):
    return lax.dot_general(left, right, (((1,), (1,)), ((), ())), preferred_element_type=f32)


def together(*values):
    return lax.optimization_barrier(values)


def in_lines(row):
    return [row[:, k : k + LANES] for k in range(0, row.shape[1], LANES)]


def start_kernel(place, hidden, offsets, *refs):
    given, table = refs[:3], refs[3]
    spread_out, own_offsets, aux, own, offset_rows, lines, sems = refs[4:]
    low = place[3] == 0
    n_dp, half, _ = spread_out.shape
    mine = hidden.at[pl.ds(pl.multiple_of(place[3] * half, half), half)]
    moves = [(mine, spread_out.at[k]) for k in range(n_dp)]
    moves += [(offsets, offset_rows)] + [(v, lines.at[k]) for k, v in enumerate(given)]
    moves += [(table, own)]
    copies = [pltpu.make_async_copy(f, t, sems.at[k]) for k, (f, t) in enumerate(moves)]
    for copy in copies:
        copy.start()
    for copy in copies[n_dp:-1]:
        copy.wait()
    piece = own_offsets.shape[0]
    values = offset_rows[...].astype(f32)
    chosen = values[:piece]
    for k in range(1, values.shape[0] // piece):
        chosen = jnp.where(place[4] == k, values[piece * k : piece * (k + 1)], chosen)
    own_offsets[...] = chosen
    rows = []
    for k in range(len(given)):
        values = lines[k]
        parts = []
        for d in range(n_dp):
            line, lane = divmod(2 * half * d, LANES)
            first = values[line : line + 1, lane : lane + half]
            second = values[line : line + 1, lane + half : lane + 2 * half]
            parts.append(jnp.where(low, first, second))
        rows.append(jnp.concatenate(parts, axis=1))
    aux[...] = jnp.concatenate(rows + [rows[0]] * 5, axis=0)
    for copy in copies[:n_dp] + copies[-1:]:
        copy.wait()


def start_call(place, start_hidden, offsets, targets_one, targets_two, advantage, table, n_dp, piece):
    own_rows, width = start_hidden.shape
    half = own_rows // 2
    lines = [v.reshape(-1, LANES) for v in (targets_one, targets_two, advantage)]
    operands = [start_hidden, offsets, *lines, table]
    return call(
        start_kernel,
        [place] + [pltpu.with_memory_space_constraint(v, pltpu.HBM) for v in operands],
        [
            jax.ShapeDtypeStruct((n_dp, half, width), bf16),
            jax.ShapeDtypeStruct((piece, width), f32),
            jax.ShapeDtypeStruct((8, n_dp * half), jnp.int32),
            pltpu.VMEM(table.shape, bf16),
        ],
        [
            pltpu.VMEM((own_rows, width), bf16),
            pltpu.VMEM((3, *lines[0].shape), jnp.int32),
            pltpu.SemaphoreType.DMA((n_dp + 5,)),
        ],
        scalars=1,
        far=range(1, 7),
    )


def logits_kernel(second, *refs):
    if second:
        pieces, own, other, lse, before, logits, stats, hidden = refs
        gather_rows(pieces, hidden)
    else:
        hidden, own, other, logits, stats, local_out = refs
    n_rows = logits.shape[1]
    block = other.shape[0]
    old = jnp.full((1, n_rows), -1e30, f32)
    total = jnp.zeros((1, n_rows), f32)
    weighted = total
    for table, base in ((own, 0), (other, block)):
        for start in range(0, block, VOCAB_TILE):
            tile = nt(table[start : start + VOCAB_TILE, :], hidden[...])
            logits[base + start : base + start + VOCAB_TILE, :] = tile
            top = jnp.maximum(old, jnp.max(tile, axis=0, keepdims=True))
            shifted = tile - top
            expo = jnp.exp(shifted)
            scale = jnp.exp(old - top)
            weighted = scale * (weighted + (old - top) * total) + jnp.sum(
                expo * shifted, axis=0, keepdims=True
            )
            total = scale * total + jnp.sum(expo, axis=0, keepdims=True)
            old = top
    log_total = old + jnp.log(total)
    mean = old + weighted / total
    lines = in_lines(log_total)
    if second:
        lines += in_lines(mean)
        lines += in_lines(jnp.exp(before[0:1, :] - lse[0:1, :]) * before[1:2, :])
    else:
        local_out[...] = jnp.concatenate([log_total, mean] + [mean] * 6, axis=0)
    lines += [jnp.zeros((1, LANES), f32)] * (stats.shape[1] - len(lines))
    stats[...] = jnp.broadcast_to(jnp.concatenate(lines, axis=0)[None], stats.shape)


def first_logits_call(hidden, table, other, n_chip):
    block, width = table.shape
    rows = hidden.shape[0]
    return call(
        functools.partial(logits_kernel, False),
        [hidden, in_vmem(table), in_vmem(other)],
        [
            pltpu.VMEM((2 * block, rows), f32),
            jax.ShapeDtypeStruct((n_chip, rows // LANES, LANES), f32),
            jax.ShapeDtypeStruct((8, rows), f32),
        ],
    )


def second_logits_call(pieces, tables, lse, before):
    block, width = tables[0].shape
    n_chip, piece, _ = pieces.shape
    rows = n_chip * piece
    return call(
        functools.partial(logits_kernel, True),
        [pieces, in_vmem(tables[0]), in_vmem(tables[1]), lse, before],
        [
            pltpu.VMEM((2 * block, rows), f32),
            jax.ShapeDtypeStruct((n_chip, 8, LANES), f32),
            jax.ShapeDtypeStruct((rows, width), bf16),
        ],
    )


def stat(stats, k, n_rows):
    n = n_rows // LANES
    return jnp.concatenate([stats[:, k * n + j, :] for j in range(n)], axis=1)


def all_lse(local_lse):
    peak = jnp.max(local_lse, axis=0, keepdims=True)
    return peak + jnp.log(jnp.sum(jnp.exp(local_lse - peak), axis=0, keepdims=True))


def logit_grad(logits, probs, mean, adv, entries, targets):
    onehot = (entries == targets).astype(f32)
    return -adv * (onehot - probs) + ENTROPY_WEIGHT * probs * (logits - mean)


def entries_of(first, n, rows):
    return first + lax.broadcasted_iota(jnp.int32, (n, rows), 0)


def mixture_kernel(with_grad, *refs):
    if with_grad:
        place, logits, stats, aux, own, other = refs[:6]
    else:
        logits, stats, own, other = refs[:4]
    coef, partial, rows, turned = refs[-4:]
    block, width = own.shape
    n_rows = logits.shape[1]
    local_lse = stat(stats, 0, n_rows)
    lse = all_lse(local_lse)
    row = lse
    if with_grad:
        adv = aux[2:3, :].astype(f32)
        weight = jnp.exp(local_lse - lse)
        mean = jnp.sum(weight * stat(stats, 1, n_rows), axis=0, keepdims=True)
        row = jnp.sum(stat(stats, 2, n_rows), axis=0, keepdims=True)
    rows[...] = jnp.broadcast_to(row, rows.shape)
    for start in range(0, 2 * block, VOCAB_TILE):
        tile = logits[start : start + VOCAB_TILE, :]
        probs = jnp.exp(tile - lse)
        if with_grad:
            entries = entries_of(place[start // block] + start % block, VOCAB_TILE, n_rows)
            probs = logit_grad(tile, probs, mean, adv, entries, aux[1:2, :])
        coef[start : start + VOCAB_TILE, :] = probs.astype(bf16)
        turned[:, start : start + VOCAB_TILE] = probs.T.astype(bf16)
    for start in range(0, width, WIDTH_TILE):
        columns = slice(start, start + WIDTH_TILE)
        value = jnp.dot(turned[:, :block], own[:, columns], preferred_element_type=f32)
        value = value + jnp.dot(turned[:, block:], other[:, columns], preferred_element_type=f32)
        scatter_rows(value, partial, start)


def mixture_call(logits, stats, tables, grad=None):
    block, width = tables[0].shape
    n_rows = logits.shape[1]
    tables = [in_vmem(t) for t in tables]
    operands = [in_vmem(logits), stats, *tables]
    if grad is not None:
        place, aux = grad
        operands = [place, in_vmem(logits), stats, aux, *tables]
    return call(
        functools.partial(mixture_kernel, grad is not None),
        operands,
        [
            jax.ShapeDtypeStruct((2 * block, n_rows), bf16),
            jax.ShapeDtypeStruct((n_rows // 4, 4, width), bf16),
            jax.ShapeDtypeStruct((8, n_rows), f32),
        ],
        [pltpu.VMEM((n_rows, 2 * block), bf16)],
        0 if grad is None else 1,
    )


def in_thirds(value):
    high = value.astype(bf16).astype(f32)
    middle = (value - high).astype(bf16).astype(f32)
    return high, middle, value - high - middle


def sum_pieces(parts):
    total = parts[0].astype(f32)
    for k in range(1, parts.shape[0]):
        total = total + parts[k].astype(f32)
    return total


def state_kernel(parts, offsets, gain, pieces, unit_out, mixed_out, rms_out):
    mixed = sum_pieces(parts)
    state = mixed + offsets[...]
    rms = jnp.sqrt(jnp.mean(state * state, axis=1, keepdims=True) + NORM_EPS)
    unit = state / rms
    unit_out[...] = unit
    mixed_out[...] = mixed
    rms_out[...] = jnp.broadcast_to(rms, rms_out.shape)
    value = (unit * gain[...]).astype(bf16)
    for k in range(pieces.shape[0]):
        pieces[k] = value


def state_call(parts, offsets, gain):
    piece, width = offsets.shape
    return call(
        state_kernel,
        [parts, offsets, gain],
        [
            jax.ShapeDtypeStruct(parts.shape, bf16),
            jax.ShapeDtypeStruct((piece, width), f32),
            jax.ShapeDtypeStruct((piece, width), f32),
            jax.ShapeDtypeStruct((piece, LANES), f32),
        ],
    )


def offset_kernel(parts, unit, mixed, rms, gain, pieces):
    piece, width = unit.shape
    scaled = sum_pieces(parts) * gain[...]
    along = jnp.mean(scaled * unit[...], axis=1, keepdims=True)
    value = ((scaled - unit[...] * along) / rms[:, :1]).astype(bf16).astype(f32)
    inner = jnp.sum(value * mixed[...], axis=1, keepdims=True)
    lane = lax.broadcasted_iota(jnp.int32, (piece, LANES), 1)
    terms = jnp.zeros((piece, LANES), f32)
    for k, term in enumerate(in_thirds(inner) + in_thirds(along) + in_thirds(rms[:, :1])):
        terms = jnp.where(lane == k, term, terms)
    line = jnp.concatenate([value, terms], axis=1).astype(bf16)
    for k in range(pieces.shape[0]):
        pieces[k] = line


def offset_call(parts, unit, mixed, rms, gain):
    n, piece, width = parts.shape
    return call(
        offset_kernel,
        [parts, unit, mixed, rms, gain],
        [jax.ShapeDtypeStruct((n, piece, width + LANES), bf16)],
    )[0]


def first_grad_kernel(half, assemble, *refs):
    if assemble:
        place, pieces, logits, lse, mean, aux, table, next_input, gain = refs[:9]
        grad, hidden, inner_out, share = refs[9:]
        n_rows, width = hidden.shape
        gather_rows(pieces, hidden)
        terms = [pieces[k, :, width:].astype(f32) for k in range(pieces.shape[0])]
        terms = jnp.concatenate(terms, axis=0)
        inner = terms.T
        inner = inner[0:1, :] + inner[1:2, :] + inner[2:3, :]
        inner_out[...] = jnp.broadcast_to(inner, inner_out.shape)
        along = terms[:, 3:4] + terms[:, 4:5] + terms[:, 5:6]
        rms = terms[:, 6:7] + terms[:, 7:8] + terms[:, 8:9]
        for start in range(0, width, WIDTH_TILE):
            columns = slice(start, start + WIDTH_TILE)
            given = next_input[:, columns].astype(f32)
            inverse = 1.0 / gain[:, columns]
            value = hidden[:, columns].astype(f32) * rms + given * inverse * along
            value = jnp.sum(value * given, axis=0, keepdims=True)
            share[:, columns] = value * inverse * inverse
    else:
        place, hidden, logits, lse, mean, aux, table, inner_in, grad = refs
        inner = inner_in[0:1, :]
    block = table.shape[0]
    adv = aux[2:3, :].astype(f32)
    for start in range(0, block, VOCAB_TILE):
        prob_grad = nt(table[start : start + VOCAB_TILE, :], hidden[...])
        tile = logits[half * block + start : half * block + start + VOCAB_TILE, :]
        probs = jnp.exp(tile - lse[0:1, :])
        entries = entries_of(place[half] + start, *tile.shape)
        value = logit_grad(tile, probs, mean[0:1, :], adv, entries, aux[0:1, :])
        value = value + probs * (prob_grad - inner)
        grad[start : start + VOCAB_TILE, :] = value.astype(bf16)


def first_grad_call(place, hidden, logits, half, lse, mean, aux, table, more):
    block, width = table.shape
    n_rows = logits.shape[1]
    out_shape = [jax.ShapeDtypeStruct((block, n_rows), bf16)]
    operands = [place, hidden, in_vmem(logits), lse, mean, aux, in_vmem(table), *more]
    assemble = hidden.ndim == 3
    if assemble:
        out_shape += [
            jax.ShapeDtypeStruct((n_rows, width), bf16),
            jax.ShapeDtypeStruct((8, n_rows), f32),
            jax.ShapeDtypeStruct((1, width), f32),
        ]
    return call(
        functools.partial(first_grad_kernel, half, assemble), operands, out_shape, (), 1
    )


def head_kernel(n, place, *refs):
    lefts, rights = refs[:n], refs[n : 2 * n]
    mine, theirs, gain_a, gain_b, head, offset, gain = refs[2 * n :]

    @pl.when(pl.program_id(0) == 0)
    def _():
        gain[...] = gain_a[...] + gain_b[...]
        half = offset.shape[0] // 2
        at = pl.ds(pl.multiple_of(place[2] * half, half), half)
        low = place[3] == 0
        offset[:half, :] = jnp.where(low, mine[at, :], theirs[at, :])
        offset[half:, :] = jnp.where(low, theirs[at, :], mine[at, :])

    tile, width = head.shape
    row = pl.ds(pl.multiple_of(pl.program_id(0) * tile, tile), tile)
    left = jnp.concatenate([r[row, :] for r in lefts], axis=1)
    for start in range(0, width, WIDTH_TILE):
        columns = slice(start, start + WIDTH_TILE)
        right = jnp.concatenate([r[:, columns] for r in rights], axis=0)
        head[:, columns] = jnp.dot(left, right, preferred_element_type=f32)


def head_call(pairs, block, place, offset_rows, offset_other, gain_a, gain_b, own_rows):
    width = pairs[0][1].shape[1]
    operands = [p[0] for p in pairs] + [p[1] for p in pairs]
    operands += [offset_rows, offset_other, gain_a, gain_b]
    return pl.pallas_call(
        functools.partial(head_kernel, len(pairs)),
        grid=(block // HEAD_TILE,),
        in_specs=[pl.BlockSpec(memory_space=pltpu.SMEM)] + [whole()] * len(operands),
        out_shape=[
            jax.ShapeDtypeStruct((block, width), f32),
            jax.ShapeDtypeStruct((own_rows, width), bf16),
            jax.ShapeDtypeStruct(gain_a.shape, f32),
        ],
        out_specs=[pl.BlockSpec((HEAD_TILE, width), lambda i: (i, 0)), whole(), whole()],
        compiler_params=pltpu.CompilerParams(vmem_limit_bytes=24 * 1024 * 1024),
    )(place, *operands)


def local(start_hidden, offsets, norm_gain, head_table, targets_one, targets_two, advantage):
    core = lax.axis_index("c")
    sub = lax.axis_index(("x", "zl"))
    n_dp = lax.axis_size(DP)
    n_chip = lax.axis_size(CHIPS)
    own_rows, width = start_hidden.shape
    half = own_rows // 2
    rows = n_dp * half
    piece = rows // n_chip
    block_rows = head_table.shape[0]

    first = (lax.axis_index(DP) * lax.axis_size(VOCAB) + lax.axis_index(VOCAB)) * block_rows
    other_first = first + (1 - 2 * core) * block_rows
    place = jnp.stack([first, other_first, lax.axis_index(DP), core, core * (half // piece) + sub])
    gain = norm_gain[None, :]

    own_half, own_offsets, aux, own = start_call(
        place, start_hidden, offsets, targets_one, targets_two, advantage, head_table, n_dp, piece
    )
    other = swap(own)
    hidden = exchange(own_half, DP).reshape(rows, width)
    hidden_other = swap(hidden)
    logits_one, stats, before = first_logits_call(hidden, own, other, n_chip)
    tables = (own, other)
    stats, hidden_other = together(stats, hidden_other)
    low, partial, lse_one = mixture_call(logits_one, exchange(stats, CHIPS), tables)
    pieces, unit, mixed, rms = state_call(exchange(partial, CHIPS), own_offsets, gain)

    pieces, low = together(exchange(pieces, CHIPS), low)
    low_other = swap(low[block_rows:])
    logits_two, stats, next_input = second_logits_call(pieces, tables, lse_one, before)
    stats, low_other = together(stats, low_other)
    stats, next_input = together(exchange(stats, CHIPS), next_input)
    next_other = swap(next_input)
    grad_two, partial, mean_one = mixture_call(logits_two, stats, tables, (place, aux))
    partial, next_other = together(partial, next_other)
    pieces = offset_call(exchange(partial, CHIPS), unit, mixed, rms, gain)
    pieces, grad_two = together(exchange(pieces, CHIPS), grad_two)
    two_other = swap(grad_two[block_rows:])

    grad_b, offset_rows, inner, share = first_grad_call(
        place, pieces, logits_one, 1, lse_one, mean_one, aux, tables[1], (next_input, gain)
    )
    one_other = swap(grad_b)
    offset_other = swap(offset_rows)
    share_other = swap(share)
    (grad_a,) = first_grad_call(
        place, offset_rows, logits_one, 0, lse_one, mean_one, aux, tables[0], (inner,)
    )
    head_grad, offset_grad, gain_grad = head_call(
        [
            (grad_two, next_input),
            (two_other, next_other),
            (low, offset_rows),
            (grad_a, hidden),
            (low_other, offset_other),
            (one_other, hidden_other),
        ],
        block_rows,
        place,
        offset_rows,
        offset_other,
        share,
        share_other,
        own_rows,
    )
    return (head_grad, gain_grad.reshape(width), offset_grad)


def solution(mesh):
    fine = Mesh(mesh.devices.reshape(2, 4, 4, 2, 2), ("zh", "y", "x", "zl", "c"))
    rows = DP + VOCAB
    return jax.shard_map(
        local,
        mesh=fine,
        in_specs=(P(DP, None), P(DP, None), P(), P(rows, None), P(), P(), P()),
        out_specs=(P(rows, None), P(), P(DP, None)),
        check_vma=False,
    )
```

```python
import functools

import jax
import jax.numpy as jnp
from jax import lax
from jax.experimental import pallas as pl
from jax.experimental.pallas import tpu as pltpu
from jax.sharding import Mesh, PartitionSpec as P

ENTROPY_WEIGHT = 0.05
NORM_EPS = 1e-05
DP = ("zh", "y")
VOCAB = ("x", "zl", "c")
CHIPS = ("zh", "y", "x", "zl")
SWAP = [(0, 1), (1, 0)]
VOCAB_TILE = 256
WIDTH_TILE = 512
HEAD_TILE = 256
LANES = 128
f32 = jnp.float32
bf16 = jnp.bfloat16


def swap(value):
    return lax.ppermute(value, "c", SWAP)


def exchange(blocks, axes):
    return lax.all_to_all(blocks, axes, 0, 0)


def whole():
    return pl.BlockSpec(memory_space=pltpu.VMEM)


def in_vmem(value):
    return pltpu.with_memory_space_constraint(value, pltpu.VMEM)


def call(kernel, operands, out_shape, scratch_shapes=(), scalars=0, vmem=16, far=()):
    specs = [pl.BlockSpec(memory_space=pltpu.SMEM)] * scalars
    specs += [whole()] * (len(operands) - scalars)
    for k in far:
        specs[k] = pl.BlockSpec(memory_space=pl.ANY)
    return pl.pallas_call(
        kernel,
        in_specs=specs,
        out_shape=out_shape,
        out_specs=[whole()] * len(out_shape),
        scratch_shapes=scratch_shapes,
        compiler_params=pltpu.CompilerParams(vmem_limit_bytes=vmem * 1024 * 1024),
    )(*operands)


def gather_rows(pieces_ref, rows_ref):
    for j in range(rows_ref.shape[0] // 16):
        part = [pieces_ref[4 * j + k].astype(f32) for k in range(4)]
        rows_ref[16 * j : 16 * j + 16, :] = jnp.concatenate(part, axis=0).astype(bf16)


def scatter_rows(value, pieces_ref, start):
    for j in range(value.shape[0] // 4):
        pieces_ref[j, :, start : start + value.shape[1]] = value[4 * j : 4 * j + 4].astype(bf16)


def nt(left, right):
    return lax.dot_general(left, right, (((1,), (1,)), ((), ())), preferred_element_type=f32)


def together(*values):
    return lax.optimization_barrier(values)


def in_lines(row):
    return [row[:, k : k + LANES] for k in range(0, row.shape[1], LANES)]


def start_kernel(place, hidden, offsets, *refs):
    given, table = refs[:3], refs[3]
    spread_out, own_offsets, aux, own, offset_rows, lines, sems = refs[4:]
    low = place[3] == 0
    n_dp, half, _ = spread_out.shape
    mine = hidden.at[pl.ds(pl.multiple_of(place[3] * half, half), half)]
    moves = [(mine, spread_out.at[k]) for k in range(n_dp)]
    moves += [(offsets, offset_rows)] + [(v, lines.at[k]) for k, v in enumerate(given)]
    moves += [(table, own)]
    copies = [pltpu.make_async_copy(f, t, sems.at[k]) for k, (f, t) in enumerate(moves)]
    for copy in copies:
        copy.start()
    for copy in copies[n_dp:-1]:
        copy.wait()
    piece = own_offsets.shape[0]
    values = offset_rows[...].astype(f32)
    chosen = values[:piece]
    for k in range(1, values.shape[0] // piece):
        chosen = jnp.where(place[4] == k, values[piece * k : piece * (k + 1)], chosen)
    own_offsets[...] = chosen
    rows = []
    for k in range(len(given)):
        values = lines[k]
        parts = []
        for d in range(n_dp):
            line, lane = divmod(2 * half * d, LANES)
            first = values[line : line + 1, lane : lane + half]
            second = values[line : line + 1, lane + half : lane + 2 * half]
            parts.append(jnp.where(low, first, second))
        rows.append(jnp.concatenate(parts, axis=1))
    aux[...] = jnp.concatenate(rows + [rows[0]] * 5, axis=0)
    for copy in copies[:n_dp] + copies[-1:]:
        copy.wait()


def start_call(place, start_hidden, offsets, targets_one, targets_two, advantage, table, n_dp, piece):
    own_rows, width = start_hidden.shape
    half = own_rows // 2
    lines = [v.reshape(-1, LANES) for v in (targets_one, targets_two, advantage)]
    operands = [start_hidden, offsets, *lines, table]
    return call(
        start_kernel,
        [place] + [pltpu.with_memory_space_constraint(v, pltpu.HBM) for v in operands],
        [
            jax.ShapeDtypeStruct((n_dp, half, width), bf16),
            jax.ShapeDtypeStruct((piece, width), f32),
            jax.ShapeDtypeStruct((8, n_dp * half), jnp.int32),
            pltpu.VMEM(table.shape, bf16),
        ],
        [
            pltpu.VMEM((own_rows, width), bf16),
            pltpu.VMEM((3, *lines[0].shape), jnp.int32),
            pltpu.SemaphoreType.DMA((n_dp + 5,)),
        ],
        scalars=1,
        far=range(1, 7),
    )


def logits_kernel(second, *refs):
    if second:
        pieces, own, other, logits, stats, hidden = refs
        gather_rows(pieces, hidden)
    else:
        hidden, own, other, logits, stats = refs
    n_rows = logits.shape[1]
    block = other.shape[0]
    old = jnp.full((1, n_rows), -1e30, f32)
    total = jnp.zeros((1, n_rows), f32)
    weighted = total
    for table, base in ((own, 0), (other, block)):
        for start in range(0, block, VOCAB_TILE):
            tile = nt(table[start : start + VOCAB_TILE, :], hidden[...])
            logits[base + start : base + start + VOCAB_TILE, :] = tile
            top = jnp.maximum(old, jnp.max(tile, axis=0, keepdims=True))
            shifted = tile - top
            expo = jnp.exp(shifted)
            scale = jnp.exp(old - top)
            weighted = scale * (weighted + (old - top) * total) + jnp.sum(
                expo * shifted, axis=0, keepdims=True
            )
            total = scale * total + jnp.sum(expo, axis=0, keepdims=True)
            old = top
    lines = in_lines(old + jnp.log(total)) + in_lines(old + weighted / total)
    stats[...] = jnp.broadcast_to(jnp.concatenate(lines, axis=0)[None], stats.shape)


def logits_call(hidden, tables, n_chip):
    block, width = tables[0].shape
    second = hidden.ndim == 3
    rows = hidden.size // width
    out_shape = [
        pltpu.VMEM((2 * block, rows), f32),
        jax.ShapeDtypeStruct((n_chip, 2 * rows // LANES, LANES), f32),
    ]
    if second:
        out_shape.append(jax.ShapeDtypeStruct((rows, width), bf16))
    return call(
        functools.partial(logits_kernel, second),
        [hidden, in_vmem(tables[0]), in_vmem(tables[1])],
        out_shape,
    )


def stat(stats, k, n_rows):
    n = n_rows // LANES
    return jnp.concatenate([stats[:, k * n + j, :] for j in range(n)], axis=1)


def all_lse(local_lse):
    peak = jnp.max(local_lse, axis=0, keepdims=True)
    return peak + jnp.log(jnp.sum(jnp.exp(local_lse - peak), axis=0, keepdims=True))


def logit_grad(logits, probs, mean, adv, entries, targets):
    onehot = (entries == targets).astype(f32)
    return -adv * (onehot - probs) + ENTROPY_WEIGHT * probs * (logits - mean)


def entries_of(first, n, rows):
    return first + lax.broadcasted_iota(jnp.int32, (n, rows), 0)


def mixture_kernel(with_grad, *refs):
    if with_grad:
        place, logits, stats, aux, own, other = refs[:6]
        coef, partial, turned = refs[6:]
    else:
        logits, stats, own, other, coef, partial, rows, turned = refs
    block, width = own.shape
    n_rows = logits.shape[1]
    local_lse = stat(stats, 0, n_rows)
    lse = all_lse(local_lse)
    weight = jnp.exp(local_lse - lse)
    mean = jnp.sum(weight * stat(stats, 1, n_rows), axis=0, keepdims=True)
    if with_grad:
        adv = aux[2:3, :].astype(f32)
    else:
        rows[...] = jnp.concatenate([lse] + [mean] * 7, axis=0)
    for start in range(0, 2 * block, VOCAB_TILE):
        tile = logits[start : start + VOCAB_TILE, :]
        probs = jnp.exp(tile - lse)
        if with_grad:
            entries = entries_of(place[start // block] + start % block, VOCAB_TILE, n_rows)
            probs = logit_grad(tile, probs, mean, adv, entries, aux[1:2, :])
        coef[start : start + VOCAB_TILE, :] = probs.astype(bf16)
        turned[:, start : start + VOCAB_TILE] = probs.T.astype(bf16)
    for start in range(0, width, WIDTH_TILE):
        columns = slice(start, start + WIDTH_TILE)
        value = jnp.dot(turned[:, :block], own[:, columns], preferred_element_type=f32)
        value = value + jnp.dot(turned[:, block:], other[:, columns], preferred_element_type=f32)
        scatter_rows(value, partial, start)


def mixture_call(logits, stats, tables, grad=None):
    block, width = tables[0].shape
    n_rows = logits.shape[1]
    tables = [in_vmem(t) for t in tables]
    operands = [in_vmem(logits), stats, *tables]
    out_shape = [
        jax.ShapeDtypeStruct((2 * block, n_rows), bf16),
        jax.ShapeDtypeStruct((n_rows // 4, 4, width), bf16),
    ]
    if grad is None:
        out_shape.append(jax.ShapeDtypeStruct((8, n_rows), f32))
    else:
        place, aux = grad
        operands = [place, in_vmem(logits), stats, aux, *tables]
    return call(
        functools.partial(mixture_kernel, grad is not None),
        operands,
        out_shape,
        [pltpu.VMEM((n_rows, 2 * block), bf16)],
        0 if grad is None else 1,
    )


def in_thirds(value):
    high = value.astype(bf16).astype(f32)
    middle = (value - high).astype(bf16).astype(f32)
    return high, middle, value - high - middle


def sum_pieces(parts):
    total = parts[0].astype(f32)
    for k in range(1, parts.shape[0]):
        total = total + parts[k].astype(f32)
    return total


def state_kernel(parts, offsets, gain, pieces, unit_out, mixed_out, rms_out):
    mixed = sum_pieces(parts)
    state = mixed + offsets[...]
    rms = jnp.sqrt(jnp.mean(state * state, axis=1, keepdims=True) + NORM_EPS)
    unit = state / rms
    unit_out[...] = unit
    mixed_out[...] = mixed
    rms_out[...] = jnp.broadcast_to(rms, rms_out.shape)
    value = (unit * gain[...]).astype(bf16)
    for k in range(pieces.shape[0]):
        pieces[k] = value


def state_call(parts, offsets, gain):
    piece, width = offsets.shape
    return call(
        state_kernel,
        [parts, offsets, gain],
        [
            jax.ShapeDtypeStruct(parts.shape, bf16),
            jax.ShapeDtypeStruct((piece, width), f32),
            jax.ShapeDtypeStruct((piece, width), f32),
            jax.ShapeDtypeStruct((piece, LANES), f32),
        ],
    )


def offset_kernel(parts, unit, mixed, rms, gain, pieces):
    piece, width = unit.shape
    scaled = sum_pieces(parts) * gain[...]
    along = jnp.mean(scaled * unit[...], axis=1, keepdims=True)
    value = ((scaled - unit[...] * along) / rms[:, :1]).astype(bf16).astype(f32)
    inner = jnp.sum(value * mixed[...], axis=1, keepdims=True)
    lane = lax.broadcasted_iota(jnp.int32, (piece, LANES), 1)
    terms = jnp.zeros((piece, LANES), f32)
    for k, term in enumerate(in_thirds(inner) + in_thirds(along) + in_thirds(rms[:, :1])):
        terms = jnp.where(lane == k, term, terms)
    line = jnp.concatenate([value, terms], axis=1).astype(bf16)
    for k in range(pieces.shape[0]):
        pieces[k] = line


def offset_call(parts, unit, mixed, rms, gain):
    n, piece, width = parts.shape
    return call(
        offset_kernel,
        [parts, unit, mixed, rms, gain],
        [jax.ShapeDtypeStruct((n, piece, width + LANES), bf16)],
    )[0]


def rows_kernel(pieces, next_input, gain, hidden, inner_out, share):
    gather_rows(pieces, hidden)
    width = share.shape[1]
    inner = hidden[:, width:].astype(f32).T
    inner = inner[0:1, :] + inner[1:2, :] + inner[2:3, :]
    inner_out[...] = jnp.broadcast_to(inner, inner_out.shape)
    for start in range(0, width, WIDTH_TILE):
        columns = slice(start, start + WIDTH_TILE)
        share[:, columns] = gain_share(hidden, next_input, gain, columns, width)


def rows_call(pieces, next_input, gain):
    n_rows, width = next_input.shape
    return call(
        rows_kernel,
        [pieces, next_input, gain],
        [
            jax.ShapeDtypeStruct((n_rows, pieces.shape[2]), bf16),
            jax.ShapeDtypeStruct((8, n_rows), f32),
            jax.ShapeDtypeStruct((1, width), f32),
        ],
    )


def first_grad_kernel(half, place, hidden, logits, rows, aux, table, inner_in, grad):
    inner = inner_in[0:1, :]
    block, width = table.shape
    adv = aux[2:3, :].astype(f32)
    lse, mean = rows[0:1, :], rows[1:2, :]
    for start in range(0, block, VOCAB_TILE):
        prob_grad = nt(table[start : start + VOCAB_TILE, :], hidden[:, :width])
        tile = logits[half * block + start : half * block + start + VOCAB_TILE, :]
        probs = jnp.exp(tile - lse)
        entries = entries_of(place[half] + start, *tile.shape)
        value = logit_grad(tile, probs, mean, adv, entries, aux[0:1, :])
        value = value + probs * (prob_grad - inner)
        grad[start : start + VOCAB_TILE, :] = value.astype(bf16)


def first_grad_call(place, hidden, logits, half, rows, aux, table, inner):
    return call(
        functools.partial(first_grad_kernel, half),
        [place, hidden, in_vmem(logits), rows, aux, in_vmem(table), inner],
        [jax.ShapeDtypeStruct((table.shape[0], logits.shape[1]), bf16)],
        (),
        1,
    )[0]


def gain_share(offset_rows, next_input, gain, columns, width):
    terms = offset_rows[:, width:].astype(f32)
    along = terms[:, 3:4] + terms[:, 4:5] + terms[:, 5:6]
    rms = terms[:, 6:7] + terms[:, 7:8] + terms[:, 8:9]
    given = next_input[:, columns].astype(f32)
    inverse = 1.0 / gain[:, columns]
    value = offset_rows[:, columns].astype(f32) * rms + given * inverse * along
    return jnp.sum(value * given, axis=0, keepdims=True) * inverse * inverse


def head_kernel(n, place, *refs):
    lefts, rights = refs[:n], refs[n : 2 * n]
    mine, theirs, share, share_other, head, offset, gain_grad = refs[2 * n :]
    tile, width = head.shape

    @pl.when(pl.program_id(0) == 0)
    def _():
        gain_grad[...] = share[...] + share_other[...]
        half = offset.shape[0] // 2
        at = pl.ds(pl.multiple_of(place[2] * half, half), half)
        low = place[3] == 0
        offset[:half, :] = jnp.where(low, mine[at, :width], theirs[at, :width])
        offset[half:, :] = jnp.where(low, theirs[at, :width], mine[at, :width])

    row = pl.ds(pl.multiple_of(pl.program_id(0) * tile, tile), tile)
    left = jnp.concatenate([r[row, :] for r in lefts], axis=1)
    for start in range(0, width, WIDTH_TILE):
        columns = slice(start, start + WIDTH_TILE)
        right = jnp.concatenate([r[:, columns] for r in rights], axis=0)
        head[:, columns] = jnp.dot(left, right, preferred_element_type=f32)


def head_call(pairs, block, place, more, own_rows):
    width = pairs[0][1].shape[1]
    operands = [p[0] for p in pairs] + [p[1] for p in pairs] + list(more)
    return pl.pallas_call(
        functools.partial(head_kernel, len(pairs)),
        grid=(block // HEAD_TILE,),
        in_specs=[pl.BlockSpec(memory_space=pltpu.SMEM)] + [whole()] * len(operands),
        out_shape=[
            jax.ShapeDtypeStruct((block, width), f32),
            jax.ShapeDtypeStruct((own_rows, width), bf16),
            jax.ShapeDtypeStruct((1, width), f32),
        ],
        out_specs=[pl.BlockSpec((HEAD_TILE, width), lambda i: (i, 0)), whole(), whole()],
        compiler_params=pltpu.CompilerParams(vmem_limit_bytes=24 * 1024 * 1024),
    )(place, *operands)


def local(start_hidden, offsets, norm_gain, head_table, targets_one, targets_two, advantage):
    core = lax.axis_index("c")
    sub = lax.axis_index(("x", "zl"))
    n_dp = lax.axis_size(DP)
    n_chip = lax.axis_size(CHIPS)
    own_rows, width = start_hidden.shape
    half = own_rows // 2
    rows = n_dp * half
    piece = rows // n_chip
    block_rows = head_table.shape[0]

    first = (lax.axis_index(DP) * lax.axis_size(VOCAB) + lax.axis_index(VOCAB)) * block_rows
    other_first = first + (1 - 2 * core) * block_rows
    place = jnp.stack([first, other_first, lax.axis_index(DP), core, core * (half // piece) + sub])
    gain = norm_gain[None, :]

    own_half, own_offsets, aux, own = start_call(
        place, start_hidden, offsets, targets_one, targets_two, advantage, head_table, n_dp, piece
    )
    tables = (own, swap(own))
    hidden = exchange(own_half, DP).reshape(rows, width)
    logits_one, stats = logits_call(hidden, tables, n_chip)
    low, partial, rows_one = mixture_call(logits_one, exchange(stats, CHIPS), tables)
    pieces, unit, mixed, rms = state_call(exchange(partial, CHIPS), own_offsets, gain)

    pieces, low, hidden = together(exchange(pieces, CHIPS), low, hidden)
    low_other = swap(low[block_rows:])
    hidden_other = swap(hidden)
    logits_two, stats, next_input = logits_call(pieces, tables, n_chip)
    stats, low_other, hidden_other = together(stats, low_other, hidden_other)
    grad_two, partial = mixture_call(
        logits_two, exchange(stats, CHIPS), tables, (place, aux)
    )
    pieces = offset_call(exchange(partial, CHIPS), unit, mixed, rms, gain)
    pieces, grad_two, next_input = together(exchange(pieces, CHIPS), grad_two, next_input)
    next_other = swap(next_input)
    two_other = swap(grad_two[block_rows:])

    offset_rows, inner, share = rows_call(pieces, next_input, gain)
    offset_other = swap(offset_rows)
    share_other = swap(share)
    grad_b = first_grad_call(
        place, offset_rows, logits_one, 1, rows_one, aux, tables[1], inner
    )
    one_other = swap(grad_b)
    inner, offset_other = together(inner, offset_other)
    grad_a = first_grad_call(
        place, offset_rows, logits_one, 0, rows_one, aux, tables[0], inner
    )
    head_grad, offset_grad, gain_grad = head_call(
        [
            (grad_two, next_input),
            (two_other, next_other),
            (low, offset_rows),
            (grad_a, hidden),
            (low_other, offset_other),
            (one_other, hidden_other),
        ],
        block_rows,
        place,
        (offset_rows, offset_other, share, share_other),
        own_rows,
    )
    return (head_grad, gain_grad.reshape(width), offset_grad)


def solution(mesh):
    fine = Mesh(mesh.devices.reshape(2, 4, 4, 2, 2), ("zh", "y", "x", "zl", "c"))
    rows = DP + VOCAB
    return jax.shard_map(
        local,
        mesh=fine,
        in_specs=(P(DP, None), P(DP, None), P(), P(rows, None), P(), P(), P()),
        out_specs=(P(rows, None), P(), P(DP, None)),
        check_vma=False,
    )
```

```python
import functools

import jax
import jax.numpy as jnp
from jax import lax
from jax.experimental import pallas as pl
from jax.experimental.pallas import tpu as pltpu
from jax.sharding import Mesh, PartitionSpec as P

ENTROPY_WEIGHT = 0.05
NORM_EPS = 1e-05
DP = ("zh", "y")
VOCAB = ("x", "zl", "c")
CHIPS = ("zh", "y", "x", "zl")
SWAP = [(0, 1), (1, 0)]
VOCAB_TILE = 256
WIDTH_TILE = 512
HEAD_TILE = 256
LANES = 128
f32 = jnp.float32
bf16 = jnp.bfloat16


def swap(value):
    return lax.ppermute(value, "c", SWAP)


def exchange(blocks, axes):
    return lax.all_to_all(blocks, axes, 0, 0)


def whole():
    return pl.BlockSpec(memory_space=pltpu.VMEM)


def in_vmem(value):
    return pltpu.with_memory_space_constraint(value, pltpu.VMEM)


def call(kernel, operands, out_shape, scratch_shapes=(), scalars=0, vmem=16, far=()):
    specs = [pl.BlockSpec(memory_space=pltpu.SMEM)] * scalars
    specs += [whole()] * (len(operands) - scalars)
    for k in far:
        specs[k] = pl.BlockSpec(memory_space=pl.ANY)
    return pl.pallas_call(
        kernel,
        in_specs=specs,
        out_shape=out_shape,
        out_specs=[whole()] * len(out_shape),
        scratch_shapes=scratch_shapes,
        compiler_params=pltpu.CompilerParams(vmem_limit_bytes=vmem * 1024 * 1024),
    )(*operands)


def gather_rows(pieces_ref, rows_ref):
    for j in range(rows_ref.shape[0] // 16):
        part = [pieces_ref[4 * j + k].astype(f32) for k in range(4)]
        rows_ref[16 * j : 16 * j + 16, :] = jnp.concatenate(part, axis=0).astype(bf16)


def scatter_rows(value, pieces_ref, start):
    for j in range(value.shape[0] // 4):
        pieces_ref[j, :, start : start + value.shape[1]] = value[4 * j : 4 * j + 4].astype(bf16)


def nt(left, right):
    return lax.dot_general(left, right, (((1,), (1,)), ((), ())), preferred_element_type=f32)


def together(*values):
    return lax.optimization_barrier(values)


def in_lines(row):
    return [row[:, k : k + LANES] for k in range(0, row.shape[1], LANES)]


def start_kernel(place, hidden, offsets, *refs):
    given, table = refs[:3], refs[3]
    spread_out, own_offsets, aux, own, offset_rows, lines, sems = refs[4:]
    low = place[3] == 0
    n_dp, half, _ = spread_out.shape
    mine = pl.ds(pl.multiple_of(place[3] * half, half), half)
    moves = [(hidden.at[mine], spread_out.at[0]), (offsets.at[mine], offset_rows)]
    moves += [(v, lines.at[k]) for k, v in enumerate(given)]
    moves += [(table, own)]
    copies = [pltpu.make_async_copy(f, t, sems.at[k]) for k, (f, t) in enumerate(moves)]
    for copy in copies:
        copy.start()
    for copy in copies[:-1]:
        copy.wait()
    for k in range(1, n_dp):
        spread_out[k] = spread_out[0]
    piece = own_offsets.shape[0]
    values = offset_rows[...].astype(f32)
    chosen = values[:piece]
    for k in range(1, values.shape[0] // piece):
        chosen = jnp.where(place[4] == place[3] * (half // piece) + k, values[piece * k : piece * (k + 1)], chosen)
    own_offsets[...] = chosen
    rows = []
    for k in range(len(given)):
        values = lines[k]
        parts = []
        for d in range(n_dp):
            line, lane = divmod(2 * half * d, LANES)
            first = values[line : line + 1, lane : lane + half]
            second = values[line : line + 1, lane + half : lane + 2 * half]
            parts.append(jnp.where(low, first, second))
        rows.append(jnp.concatenate(parts, axis=1))
    aux[...] = jnp.concatenate(rows + [rows[0]] * 5, axis=0)
    copies[-1].wait()


def start_call(place, start_hidden, offsets, targets_one, targets_two, advantage, table, n_dp, piece):
    own_rows, width = start_hidden.shape
    half = own_rows // 2
    lines = [v.reshape(-1, LANES) for v in (targets_one, targets_two, advantage)]
    operands = [start_hidden, offsets, *lines, table]
    return call(
        start_kernel,
        [place] + [pltpu.with_memory_space_constraint(v, pltpu.HBM) for v in operands],
        [
            jax.ShapeDtypeStruct((n_dp, half, width), bf16),
            jax.ShapeDtypeStruct((piece, width), f32),
            jax.ShapeDtypeStruct((8, n_dp * half), jnp.int32),
            pltpu.VMEM(table.shape, bf16),
        ],
        [
            pltpu.VMEM((half, width), bf16),
            pltpu.VMEM((3, *lines[0].shape), jnp.int32),
            pltpu.SemaphoreType.DMA((6,)),
        ],
        scalars=1,
        far=range(1, 7),
    )


def logits_kernel(second, *refs):
    if second:
        pieces, own, other, logits, stats, hidden = refs
        gather_rows(pieces, hidden)
    else:
        hidden, own, other, logits, stats = refs
    n_rows = logits.shape[1]
    block = other.shape[0]
    old = jnp.full((1, n_rows), -1e30, f32)
    total = jnp.zeros((1, n_rows), f32)
    weighted = total
    for table, base in ((own, 0), (other, block)):
        for start in range(0, block, VOCAB_TILE):
            tile = nt(table[start : start + VOCAB_TILE, :], hidden[...])
            logits[base + start : base + start + VOCAB_TILE, :] = tile
            top = jnp.maximum(old, jnp.max(tile, axis=0, keepdims=True))
            shifted = tile - top
            expo = jnp.exp(shifted)
            scale = jnp.exp(old - top)
            weighted = scale * (weighted + (old - top) * total) + jnp.sum(
                expo * shifted, axis=0, keepdims=True
            )
            total = scale * total + jnp.sum(expo, axis=0, keepdims=True)
            old = top
    lines = in_lines(old + jnp.log(total)) + in_lines(old + weighted / total)
    stats[...] = jnp.broadcast_to(jnp.concatenate(lines, axis=0)[None], stats.shape)


def logits_call(hidden, tables, n_chip):
    block, width = tables[0].shape
    second = hidden.ndim == 3
    rows = hidden.size // width
    out_shape = [
        pltpu.VMEM((2 * block, rows), f32),
        jax.ShapeDtypeStruct((n_chip, 2 * rows // LANES, LANES), f32),
    ]
    if second:
        out_shape.append(jax.ShapeDtypeStruct((rows, width), bf16))
    return call(
        functools.partial(logits_kernel, second),
        [hidden, in_vmem(tables[0]), in_vmem(tables[1])],
        out_shape,
    )


def stat(stats, k, n_rows):
    n = n_rows // LANES
    return jnp.concatenate([stats[:, k * n + j, :] for j in range(n)], axis=1)


def all_lse(local_lse):
    peak = jnp.max(local_lse, axis=0, keepdims=True)
    return peak + jnp.log(jnp.sum(jnp.exp(local_lse - peak), axis=0, keepdims=True))


def logit_grad(logits, probs, mean, adv, entries, targets):
    onehot = (entries == targets).astype(f32)
    return -adv * (onehot - probs) + ENTROPY_WEIGHT * probs * (logits - mean)


def entries_of(first, n, rows):
    return first + lax.broadcasted_iota(jnp.int32, (n, rows), 0)


def mixture_kernel(with_grad, *refs):
    if with_grad:
        place, logits, stats, aux, own, other = refs[:6]
        coef, partial, turned = refs[6:]
    else:
        logits, stats, own, other, coef, partial, rows, turned = refs
    block, width = own.shape
    n_rows = logits.shape[1]
    local_lse = stat(stats, 0, n_rows)
    lse = all_lse(local_lse)
    weight = jnp.exp(local_lse - lse)
    mean = jnp.sum(weight * stat(stats, 1, n_rows), axis=0, keepdims=True)
    if with_grad:
        adv = aux[2:3, :].astype(f32)
    else:
        rows[...] = jnp.concatenate([lse] + [mean] * 7, axis=0)
    for start in range(0, 2 * block, VOCAB_TILE):
        tile = logits[start : start + VOCAB_TILE, :]
        probs = jnp.exp(tile - lse)
        if with_grad:
            entries = entries_of(place[start // block] + start % block, VOCAB_TILE, n_rows)
            probs = logit_grad(tile, probs, mean, adv, entries, aux[1:2, :])
        coef[start : start + VOCAB_TILE, :] = probs.astype(bf16)
        turned[:, start : start + VOCAB_TILE] = probs.T.astype(bf16)
    for start in range(0, width, WIDTH_TILE):
        columns = slice(start, start + WIDTH_TILE)
        value = jnp.dot(turned[:, :block], own[:, columns], preferred_element_type=f32)
        value = value + jnp.dot(turned[:, block:], other[:, columns], preferred_element_type=f32)
        scatter_rows(value, partial, start)


def mixture_call(logits, stats, tables, grad=None):
    block, width = tables[0].shape
    n_rows = logits.shape[1]
    tables = [in_vmem(t) for t in tables]
    operands = [in_vmem(logits), stats, *tables]
    out_shape = [
        jax.ShapeDtypeStruct((2 * block, n_rows), bf16),
        jax.ShapeDtypeStruct((n_rows // 4, 4, width), bf16),
    ]
    if grad is None:
        out_shape.append(jax.ShapeDtypeStruct((8, n_rows), f32))
    else:
        place, aux = grad
        operands = [place, in_vmem(logits), stats, aux, *tables]
    return call(
        functools.partial(mixture_kernel, grad is not None),
        operands,
        out_shape,
        [pltpu.VMEM((n_rows, 2 * block), bf16)],
        0 if grad is None else 1,
    )


def in_thirds(value):
    high = value.astype(bf16).astype(f32)
    middle = (value - high).astype(bf16).astype(f32)
    return high, middle, value - high - middle


def sum_pieces(parts):
    total = parts[0].astype(f32)
    for k in range(1, parts.shape[0]):
        total = total + parts[k].astype(f32)
    return total


def state_kernel(parts, offsets, gain, pieces, unit_out, mixed_out, rms_out):
    mixed = sum_pieces(parts)
    state = mixed + offsets[...]
    rms = jnp.sqrt(jnp.mean(state * state, axis=1, keepdims=True) + NORM_EPS)
    unit = state / rms
    unit_out[...] = unit
    mixed_out[...] = mixed
    rms_out[...] = jnp.broadcast_to(rms, rms_out.shape)
    value = (unit * gain[...]).astype(bf16)
    for k in range(pieces.shape[0]):
        pieces[k] = value


def state_call(parts, offsets, gain):
    piece, width = offsets.shape
    return call(
        state_kernel,
        [parts, offsets, gain],
        [
            jax.ShapeDtypeStruct(parts.shape, bf16),
            jax.ShapeDtypeStruct((piece, width), f32),
            jax.ShapeDtypeStruct((piece, width), f32),
            jax.ShapeDtypeStruct((piece, LANES), f32),
        ],
    )


def offset_kernel(parts, unit, mixed, rms, gain, pieces):
    piece, width = unit.shape
    scaled = sum_pieces(parts) * gain[...]
    along = jnp.mean(scaled * unit[...], axis=1, keepdims=True)
    value = ((scaled - unit[...] * along) / rms[:, :1]).astype(bf16).astype(f32)
    inner = jnp.sum(value * mixed[...], axis=1, keepdims=True)
    lane = lax.broadcasted_iota(jnp.int32, (piece, LANES), 1)
    terms = jnp.zeros((piece, LANES), f32)
    for k, term in enumerate(in_thirds(inner) + in_thirds(along) + in_thirds(rms[:, :1])):
        terms = jnp.where(lane == k, term, terms)
    line = jnp.concatenate([value, terms], axis=1).astype(bf16)
    for k in range(pieces.shape[0]):
        pieces[k] = line


def offset_call(parts, unit, mixed, rms, gain):
    n, piece, width = parts.shape
    return call(
        offset_kernel,
        [parts, unit, mixed, rms, gain],
        [jax.ShapeDtypeStruct((n, piece, width + LANES), bf16)],
    )[0]


def rows_kernel(pieces, next_input, gain, hidden, inner_out, share):
    gather_rows(pieces, hidden)
    width = share.shape[1]
    inner = hidden[:, width:].astype(f32).T
    inner = inner[0:1, :] + inner[1:2, :] + inner[2:3, :]
    inner_out[...] = jnp.broadcast_to(inner, inner_out.shape)
    for start in range(0, width, WIDTH_TILE):
        columns = slice(start, start + WIDTH_TILE)
        share[:, columns] = gain_share(hidden, next_input, gain, columns, width)


def rows_call(pieces, next_input, gain):
    n_rows, width = next_input.shape
    return call(
        rows_kernel,
        [pieces, next_input, gain],
        [
            jax.ShapeDtypeStruct((n_rows, pieces.shape[2]), bf16),
            jax.ShapeDtypeStruct((8, n_rows), f32),
            jax.ShapeDtypeStruct((1, width), f32),
        ],
    )


def first_grad_kernel(half, place, hidden, logits, rows, aux, table, inner_in, grad):
    inner = inner_in[0:1, :]
    block, width = table.shape
    adv = aux[2:3, :].astype(f32)
    lse, mean = rows[0:1, :], rows[1:2, :]
    for start in range(0, block, VOCAB_TILE):
        prob_grad = nt(table[start : start + VOCAB_TILE, :], hidden[:, :width])
        tile = logits[half * block + start : half * block + start + VOCAB_TILE, :]
        probs = jnp.exp(tile - lse)
        entries = entries_of(place[half] + start, *tile.shape)
        value = logit_grad(tile, probs, mean, adv, entries, aux[0:1, :])
        value = value + probs * (prob_grad - inner)
        grad[start : start + VOCAB_TILE, :] = value.astype(bf16)


def first_grad_call(place, hidden, logits, half, rows, aux, table, inner):
    return call(
        functools.partial(first_grad_kernel, half),
        [place, hidden, in_vmem(logits), rows, aux, in_vmem(table), inner],
        [jax.ShapeDtypeStruct((table.shape[0], logits.shape[1]), bf16)],
        (),
        1,
    )[0]


def gain_share(offset_rows, next_input, gain, columns, width):
    terms = offset_rows[:, width:].astype(f32)
    along = terms[:, 3:4] + terms[:, 4:5] + terms[:, 5:6]
    rms = terms[:, 6:7] + terms[:, 7:8] + terms[:, 8:9]
    given = next_input[:, columns].astype(f32)
    inverse = 1.0 / gain[:, columns]
    value = offset_rows[:, columns].astype(f32) * rms + given * inverse * along
    return jnp.sum(value * given, axis=0, keepdims=True) * inverse * inverse


def head_kernel(n, place, *refs):
    lefts, rights = refs[:n], refs[n : 2 * n]
    mine, theirs, share, share_other, head, offset, gain_grad = refs[2 * n :]
    tile, width = head.shape

    @pl.when(pl.program_id(0) == 0)
    def _():
        gain_grad[...] = share[...] + share_other[...]
        half = offset.shape[0] // 2
        at = pl.ds(pl.multiple_of(place[2] * half, half), half)
        low = place[3] == 0
        offset[:half, :] = jnp.where(low, mine[at, :width], theirs[at, :width])
        offset[half:, :] = jnp.where(low, theirs[at, :width], mine[at, :width])

    row = pl.ds(pl.multiple_of(pl.program_id(0) * tile, tile), tile)
    left = jnp.concatenate([r[row, :] for r in lefts], axis=1)
    for start in range(0, width, WIDTH_TILE):
        columns = slice(start, start + WIDTH_TILE)
        right = jnp.concatenate([r[:, columns] for r in rights], axis=0)
        head[:, columns] = jnp.dot(left, right, preferred_element_type=f32)


def head_call(pairs, block, place, more, own_rows):
    width = pairs[0][1].shape[1]
    operands = [p[0] for p in pairs] + [p[1] for p in pairs] + list(more)
    return pl.pallas_call(
        functools.partial(head_kernel, len(pairs)),
        grid=(block // HEAD_TILE,),
        in_specs=[pl.BlockSpec(memory_space=pltpu.SMEM)] + [whole()] * len(operands),
        out_shape=[
            jax.ShapeDtypeStruct((block, width), f32),
            jax.ShapeDtypeStruct((own_rows, width), bf16),
            jax.ShapeDtypeStruct((1, width), f32),
        ],
        out_specs=[pl.BlockSpec((HEAD_TILE, width), lambda i: (i, 0)), whole(), whole()],
        compiler_params=pltpu.CompilerParams(vmem_limit_bytes=24 * 1024 * 1024),
    )(place, *operands)


def local(start_hidden, offsets, norm_gain, head_table, targets_one, targets_two, advantage):
    core = lax.axis_index("c")
    sub = lax.axis_index(("x", "zl"))
    n_dp = lax.axis_size(DP)
    n_chip = lax.axis_size(CHIPS)
    own_rows, width = start_hidden.shape
    half = own_rows // 2
    rows = n_dp * half
    piece = rows // n_chip
    block_rows = head_table.shape[0]

    first = (lax.axis_index(DP) * lax.axis_size(VOCAB) + lax.axis_index(VOCAB)) * block_rows
    other_first = first + (1 - 2 * core) * block_rows
    place = jnp.stack([first, other_first, lax.axis_index(DP), core, core * (half // piece) + sub])
    gain = norm_gain[None, :]

    own_half, own_offsets, aux, own = start_call(
        place, start_hidden, offsets, targets_one, targets_two, advantage, head_table, n_dp, piece
    )
    tables = (own, swap(own))
    hidden = exchange(own_half, DP).reshape(rows, width)
    logits_one, stats = logits_call(hidden, tables, n_chip)
    low, partial, rows_one = mixture_call(logits_one, exchange(stats, CHIPS), tables)
    pieces, unit, mixed, rms = state_call(exchange(partial, CHIPS), own_offsets, gain)

    pieces, low, hidden = together(exchange(pieces, CHIPS), low, hidden)
    low_other = swap(low[block_rows:])
    hidden_other = swap(hidden)
    logits_two, stats, next_input = logits_call(pieces, tables, n_chip)
    stats, low_other, hidden_other = together(stats, low_other, hidden_other)
    grad_two, partial = mixture_call(
        logits_two, exchange(stats, CHIPS), tables, (place, aux)
    )
    pieces = offset_call(exchange(partial, CHIPS), unit, mixed, rms, gain)
    pieces, grad_two, next_input = together(exchange(pieces, CHIPS), grad_two, next_input)
    next_other = swap(next_input)
    two_other = swap(grad_two[block_rows:])

    offset_rows, inner, share = rows_call(pieces, next_input, gain)
    offset_other = swap(offset_rows)
    share_other = swap(share)
    grad_b = first_grad_call(
        place, offset_rows, logits_one, 1, rows_one, aux, tables[1], inner
    )
    one_other = swap(grad_b)
    inner, offset_other = together(inner, offset_other)
    grad_a = first_grad_call(
        place, offset_rows, logits_one, 0, rows_one, aux, tables[0], inner
    )
    head_grad, offset_grad, gain_grad = head_call(
        [
            (grad_two, next_input),
            (two_other, next_other),
            (low, offset_rows),
            (grad_a, hidden),
            (low_other, offset_other),
            (one_other, hidden_other),
        ],
        block_rows,
        place,
        (offset_rows, offset_other, share, share_other),
        own_rows,
    )
    return (head_grad, gain_grad.reshape(width), offset_grad)


def solution(mesh):
    fine = Mesh(mesh.devices.reshape(2, 4, 4, 2, 2), ("zh", "y", "x", "zl", "c"))
    rows = DP + VOCAB
    return jax.shard_map(
        local,
        mesh=fine,
        in_specs=(P(DP, None), P(DP, None), P(), P(rows, None), P(), P(), P()),
        out_specs=(P(rows, None), P(), P(DP, None)),
        check_vma=False,
    )
```
